32 devices in a mesh: grp: 2 (over x), ctx: 4 (over y, core), head: 4 (over z).
Axes of the slice: x: 2, y: 2, z: 4, core: 2. Of those that a mesh axis runs over, the one named last changes fastest.
Arguments:
- queries: bfloat16 [8192, 4096], P(('grp', 'ctx'), 'head'), parts along dimension 0, may hold values from -6 to 6
- keys: bfloat16 [8192, 4096], P(('grp', 'ctx'), 'head'), parts along dimension 0, may hold values from -6 to 6
- values: bfloat16 [8192, 4096], P(('grp', 'ctx'), 'head'), parts along dimension 0, may hold values from -6 to 6
- init_state: float32 [64, 128, 128], P(('grp', 'head')), parts along dimension 0, may hold values from -192 to 192
- out_grad: bfloat16 [8192, 4096], P(('grp', 'ctx'), 'head'), parts along dimension 0, may hold values from -6 to 6
Outputs:
- output: bfloat16 [8192, 4096], P(('grp', 'ctx'), 'head'), parts along dimension 0
- query_grad: bfloat16 [8192, 4096], P(('grp', 'ctx'), 'head'), parts along dimension 0
- key_grad: bfloat16 [8192, 4096], P(('grp', 'ctx'), 'head'), parts along dimension 0
- value_grad: bfloat16 [8192, 4096], P(('grp', 'ctx'), 'head'), parts along dimension 0
- state_grad: float32 [64, 128, 128], P(('grp', 'head')), parts along dimension 0
The draws below stay inside these ranges and needn't reach their ends.
There are 2 independent parts, one for each index of `grp`. The reference program is written for one: setup_inputs(seed, part) draws one part's arguments, and reference() takes and returns one part's arrays. A program takes and returns all parts, laid end to end along the dimension named above; each array names one. Nothing has to cross between parts.
All inputs are finite; a program needn't handle non-finite values.
Results may differ from the reference program's by a relative error of at most 0.0058.
Values sent between devices are 32-bit elements; how exact they have to be, the bound alone decides.
No kernel may reach another device: no remote copies, remote signals or barrier semaphores. Data moves between devices by JAX's collectives and lax.ppermute only.
A program may use at most 128 MiB of HBM per device.

```python
import jax
import jax.numpy as jnp
from jax import lax

HEADS = 32
HEAD_DIM = 128
TOK_DEV = 1024
WIDTH = 4096
TOKENS = 4096


def steps_of(own_key, extent, shards, low, largest):
    def one(axis_at, blocks):
        heights = jax.random.uniform(jax.random.fold_in(jax.random.fold_in(own_key, 6), axis_at), (blocks,), jnp.float32, low / len(shards), largest / len(shards))
        return jnp.repeat(jnp.exp(heights), extent[axis_at] // blocks).reshape((-1,) + (1,) * (len(extent) - axis_at - 1))

    level = one(*shards[0])
    for cut in shards[1:]:
        level = level * one(*cut)
    return level


def centred(key, shape, scale, reach, shards=(), kind=jnp.bfloat16):
    level = steps_of(key, shape, shards, -0.22, 0.18) if shards else 1.0
    drawn = jax.random.normal(key, shape, jnp.float32) * scale * level
    return jnp.minimum(jnp.maximum(drawn, -reach), reach).astype(kind)


def setup_inputs(seed: int = 0, part: int = 0) -> dict:
    key_of = jax.random.split(jax.random.key(seed), 6)
    own_keys = jax.random.split(jax.random.fold_in(key_of[5], part), 6)
    return {
        "queries": centred(own_keys[0], (TOKENS, WIDTH), 1.0, 6.0, ((0, 4), (1, 4))),
        "keys": centred(own_keys[1], (TOKENS, WIDTH), 1.0, 6.0, ((0, 4), (1, 4))),
        "values": centred(own_keys[2], (TOKENS, WIDTH), 1.0, 6.0, ((0, 4), (1, 4))),
        "init_state": centred(own_keys[3], (HEADS, HEAD_DIM, HEAD_DIM), (max(1, TOK_DEV // 32)), 192.0, ((0, 4),), jnp.float32),
        "out_grad": centred(own_keys[4], (TOKENS, WIDTH), 1.0, 6.0, ((0, 4), (1, 4))),
    }


def round_half(x):
    return lax.optimization_barrier(x.astype(jnp.bfloat16)).astype(jnp.float32)

def reference(queries, keys, values, init_state, out_grad):
    blocks = queries.shape[0] // TOK_DEV
    shape = (blocks, TOK_DEV, HEADS, HEAD_DIM)
    q_all = queries.astype(jnp.float32).reshape(shape)
    k_all = keys.astype(jnp.float32).reshape(shape)
    v_all = values.astype(jnp.float32).reshape(shape)
    g_all = out_grad.astype(jnp.float32).reshape(shape)
    causal = jnp.arange(TOK_DEV)[:, None] >= jnp.arange(TOK_DEV)[None, :]
    block_state = jnp.einsum('cthd,cthe->chde', k_all, v_all)
    zero_state = jnp.zeros((1, HEADS, HEAD_DIM, HEAD_DIM), jnp.float32)
    earlier = jnp.concatenate([zero_state, jnp.cumsum(block_state, axis=0)[:-1]], axis=0)
    prefix_b = round_half(init_state[None] + earlier)

    def forward_block(items):
        q_blk, k_blk, v_blk, p_blk, g_blk = items
        raw = jnp.einsum('thd,shd->hts', q_blk, k_blk)
        scores = round_half(jnp.where(causal[None], raw, 0.0))
        attended = jnp.einsum('thd,hde->the', q_blk, p_blk) + jnp.einsum('hts,she->the', scores, v_blk)
        inv_rms = lax.rsqrt(lax.optimization_barrier(jnp.mean(attended * attended, axis=-1, keepdims=True)) + 1e-06)
        normed = attended * inv_rms
        grad_att = round_half(inv_rms * (g_blk - normed * lax.optimization_barrier(jnp.mean(g_blk * normed, axis=-1, keepdims=True))))
        block_grad = jnp.einsum('thd,the->hde', q_blk, grad_att)
        return (normed.astype(jnp.bfloat16), grad_att, block_grad)
    output, grad_att, block_grad = lax.map(forward_block, (q_all, k_all, v_all, prefix_b, g_all))
    later = jnp.concatenate([jnp.cumsum(block_grad[::-1], axis=0)[::-1][1:], zero_state], axis=0)
    suffix_b = round_half(later)
    state_grad = lax.optimization_barrier(jnp.sum(block_grad, axis=0))

    def backward_block(items):
        q_blk, k_blk, v_blk, p_blk, s_blk, d_blk = items
        raw = jnp.einsum('thd,shd->hts', q_blk, k_blk)
        scores = round_half(jnp.where(causal[None], raw, 0.0))
        grad_scores = round_half(jnp.where(causal[None], jnp.einsum('the,she->hts', d_blk, v_blk), 0.0))
        q_grad = jnp.einsum('the,hde->thd', d_blk, p_blk) + jnp.einsum('hts,shd->thd', grad_scores, k_blk)
        k_grad = jnp.einsum('hts,thd->shd', grad_scores, q_blk) + jnp.einsum('she,hde->shd', v_blk, s_blk)
        v_grad = jnp.einsum('hts,the->she', scores, d_blk) + jnp.einsum('shd,hde->she', k_blk, s_blk)
        return (q_grad.astype(jnp.bfloat16), k_grad.astype(jnp.bfloat16), v_grad.astype(jnp.bfloat16))
    query_grad, key_grad, value_grad = lax.map(backward_block, (q_all, k_all, v_all, prefix_b, suffix_b, grad_att))
    flat = (blocks * TOK_DEV, HEADS * HEAD_DIM)
    return (output.reshape(flat), query_grad.reshape(flat), key_grad.reshape(flat), value_grad.reshape(flat), state_grad)
```

```python
import functools

import jax
import jax.numpy as jnp
from jax import lax
from jax.experimental import pallas as pl
from jax.experimental.pallas import tpu as pltpu
from jax.sharding import PartitionSpec as P

F32 = jnp.float32
BF16 = jnp.bfloat16
EPS = 1e-06


def mm(a, b):
    return lax.dot_general(a, b, (((1,), (0,)), ((), ())), preferred_element_type=F32)


def mm_rt(a, b):
    return lax.dot_general(a, b, (((1,), (1,)), ((), ())), preferred_element_type=F32)


def mm_lt(a, b):
    return lax.dot_general(a, b, (((0,), (0,)), ((), ())), preferred_element_type=F32)


def chunk_of(rows):
    return 256 if rows % 256 == 0 else rows


def params(mib):
    return pltpu.CompilerParams(vmem_limit_bytes=mib * 1024 * 1024)


def state_kernel(dim, size, k_ref, v_ref, total_ref, before_ref):
    heads = total_ref.shape[0]
    for h in range(heads):
        cols = slice(h * dim, (h + 1) * dim)
        run = None
        for c in range(k_ref.shape[0] // size):
            rows = slice(c * size, (c + 1) * size)
            before_ref[h, c] = jnp.zeros((dim, dim), BF16) if run is None else run.astype(BF16)
            term = mm_lt(k_ref[rows, cols], v_ref[rows, cols])
            run = term if run is None else run + term
        total_ref[h] = run


def inner_kernel(dim, size, q_ref, k_ref, v_ref, before_ref, att_ref):
    heads = before_ref.shape[0]
    keep = lax.broadcasted_iota(jnp.int32, (size, size), 0) >= lax.broadcasted_iota(
        jnp.int32, (size, size), 1
    )
    for h in range(heads):
        cols = slice(h * dim, (h + 1) * dim)
        for c in range(q_ref.shape[0] // size):
            rows = slice(c * size, (c + 1) * size)
            q, k, v = q_ref[rows, cols], k_ref[rows, cols], v_ref[rows, cols]
            scores = jnp.where(keep, mm_rt(q, k), 0.0).astype(BF16)
            att = mm(scores, v)
            if c > 0:
                att = att + mm(q, before_ref[h, c])
            att_ref[rows, cols] = att


def norm_kernel(
    dim, size, att_ref, q_ref, g_ref, prefix_ref, out_ref, ga_ref, total_ref, after_ref
):
    heads = prefix_ref.shape[0]
    for h in range(heads):
        cols = slice(h * dim, (h + 1) * dim)
        prefix = prefix_ref[h]
        run = None
        for c in reversed(range(q_ref.shape[0] // size)):
            rows = slice(c * size, (c + 1) * size)
            q = q_ref[rows, cols]
            att = att_ref[rows, cols] + mm(q, prefix)
            inv = lax.rsqrt(jnp.mean(att * att, axis=-1, keepdims=True) + EPS)
            normed = att * inv
            out_ref[rows, cols] = normed.astype(BF16)
            up = g_ref[rows, cols].astype(F32)
            along = jnp.mean(up * normed, axis=-1, keepdims=True)
            ga = (inv * (up - normed * along)).astype(BF16)
            ga_ref[rows, cols] = ga
            after_ref[h, c] = jnp.zeros((dim, dim), BF16) if run is None else run.astype(BF16)
            term = mm_lt(q, ga)
            run = term if run is None else run + term
        total_ref[h] = run


def back_kernel(
    dim, size, q_ref, k_ref, v_ref, ga_ref, prefix_ref, before_ref, after_ref, qg_ref, kg_ref, vg_ref
):
    heads = prefix_ref.shape[0]
    row = lax.broadcasted_iota(jnp.int32, (size, size), 0)
    col = lax.broadcasted_iota(jnp.int32, (size, size), 1)
    keep, keep_t = row >= col, row <= col
    chunks = q_ref.shape[0] // size
    for h in range(heads):
        cols = slice(h * dim, (h + 1) * dim)
        prefix = prefix_ref[h]
        for c in range(chunks):
            rows = slice(c * size, (c + 1) * size)
            q, k, v, ga = q_ref[rows, cols], k_ref[rows, cols], v_ref[rows, cols], ga_ref[rows, cols]
            grad = jnp.where(keep, mm_rt(ga, v), 0.0).astype(BF16)
            qg = mm(grad, k) + mm_rt(ga, prefix)
            if c > 0:
                qg = qg + mm_rt(ga, before_ref[h, c])
            qg_ref[rows, cols] = qg.astype(BF16)
            scores_t = jnp.where(keep_t, mm_rt(k, q), 0.0).astype(BF16)
            vg = mm(scores_t, ga)
            kg = mm_lt(grad, q)
            if c < chunks - 1:
                after = after_ref[h, c]
                vg = vg + mm(k, after)
                kg = kg + mm_rt(v, after)
            vg_ref[rows, cols] = vg
            kg_ref[rows, cols] = kg


def last_kernel(dim, k_ref, v_ref, suffix_ref, kp_ref, vp_ref, kg_ref, vg_ref):
    for h in range(suffix_ref.shape[0]):
        cols = slice(h * dim, (h + 1) * dim)
        suffix = suffix_ref[h]
        kg_ref[:, cols] = (kp_ref[:, cols] + mm_rt(v_ref[:, cols], suffix)).astype(BF16)
        vg_ref[:, cols] = (vp_ref[:, cols] + mm(k_ref[:, cols], suffix)).astype(BF16)


def across(own, n):
    place = lax.axis_index("ctx")
    if n % 2 or own.shape[0] % 2:
        every = lax.all_gather(own, "ctx", axis=0)
        order = jnp.arange(n)[:, None, None, None]
        return (
            jnp.sum(jnp.where(order < place, every, 0.0), axis=0),
            jnp.sum(jnp.where(order > place, every, 0.0), axis=0),
        )
    half, pairs = own.shape[0] // 2, n // 2
    first = place % 2 == 0
    pair = place // 2
    swap = [(i, i ^ 1) for i in range(n)]
    shift = [(i, (i + 2) % n) for i in range(n)]
    near = lax.ppermute(own, "ctx", swap)
    both = own + near
    mine = jnp.where(first, both[:half], both[half:])
    moving, far = mine, []
    for _ in range(pairs - 1):
        moving = lax.ppermute(moving, "ctx", shift)
        far.append(moving)
    earlier, later = jnp.zeros_like(own), jnp.zeros_like(own)
    if pairs == 2:
        other = lax.ppermute(far[0], "ctx", swap)
        full = jnp.where(
            first, jnp.concatenate([far[0], other]), jnp.concatenate([other, far[0]])
        )
        earlier, later = jnp.where(pair > 0, full, 0.0), jnp.where(pair > 0, 0.0, full)
    elif pairs > 2:
        low = sum(jnp.where(pair >= j + 1, r, 0.0) for j, r in enumerate(far))
        high = sum(jnp.where(pair >= j + 1, 0.0, r) for j, r in enumerate(far))
        sums = jnp.stack([low, high])
        other = lax.ppermute(sums, "ctx", swap)
        full = jnp.where(
            first, jnp.concatenate([sums, other], 1), jnp.concatenate([other, sums], 1)
        )
        earlier, later = full[0], full[1]
    return earlier + jnp.where(first, 0.0, near), later + jnp.where(first, near, 0.0)


def shards(n, queries, keys, values, init_state, out_grad):
    rows, width = queries.shape
    heads, dim = init_state.shape[:2]
    size = chunk_of(rows)
    chunks = rows // size
    per = 2 if heads % 2 == 0 else 1
    grid = (heads // per,)
    tall = pl.BlockSpec((rows, per * dim), lambda i: (0, i))
    state = pl.BlockSpec((per, dim, dim), lambda i: (i, 0, 0))
    states = pl.BlockSpec((per, chunks, dim, dim), lambda i: (i, 0, 0, 0))
    tall_b = jax.ShapeDtypeStruct((rows, width), BF16)
    tall_f = jax.ShapeDtypeStruct((rows, width), F32)
    state_f = jax.ShapeDtypeStruct((heads, dim, dim), F32)
    states_b = jax.ShapeDtypeStruct((heads, chunks, dim, dim), BF16)
    small = 2 * heads * rows * dim * dim
    square = 2 * heads * rows * size * dim

    def call(body, name, ins, outs, flops, nbytes, mib=16):
        return pl.pallas_call(
            body,
            grid=grid,
            in_specs=[s for s in ins],
            out_specs=[s for s, _ in outs],
            out_shape=[t for _, t in outs],
            compiler_params=params(mib),
            cost_estimate=pl.CostEstimate(flops=flops, bytes_accessed=nbytes, transcendentals=0),
            name=name,
        )

    piece = rows * width * 2
    block_state, before = call(
        functools.partial(state_kernel, dim, size),
        "states",
        [tall, tall],
        [(state, state_f), (states, states_b)],
        small,
        2 * piece,
    )(keys, values)
    (inner,) = call(
        functools.partial(inner_kernel, dim, size),
        "inner",
        [tall, tall, tall, states],
        [(tall, tall_f)],
        2 * square + small,
        5 * piece,
    )(queries, keys, values, before)
    earlier, _ = across(block_state, n)
    prefix_b = (init_state + earlier).astype(BF16)
    output, grad_att, block_grad, after = call(
        functools.partial(norm_kernel, dim, size),
        "norm",
        [tall, tall, tall, state],
        [(tall, tall_b), (tall, tall_b), (state, state_f), (states, states_b)],
        2 * small,
        6 * piece,
    )(inner, queries, out_grad, prefix_b)
    earlier_grad, later_grad = across(block_grad, n)
    state_grad = earlier_grad + block_grad + later_grad
    suffix_b = later_grad.astype(BF16)
    query_grad, key_part, value_part = call(
        functools.partial(back_kernel, dim, size),
        "back",
        [tall, tall, tall, tall, state, states, states],
        [(tall, tall_b), (tall, tall_f), (tall, tall_f)],
        5 * square + 3 * small,
        9 * piece,
        24,
    )(queries, keys, values, grad_att, prefix_b, before, after)
    key_grad, value_grad = call(
        functools.partial(last_kernel, dim),
        "last",
        [tall, tall, state, tall, tall],
        [(tall, tall_b), (tall, tall_b)],
        2 * small,
        8 * piece,
    )(keys, values, suffix_b, key_part, value_part)
    return output, query_grad, key_grad, value_grad, state_grad


def solution(mesh):
    wide = P(("grp", "ctx"), "head")
    deep = P(("grp", "head"), None, None)
    return jax.shard_map(
        functools.partial(shards, mesh.shape["ctx"]),
        mesh=mesh,
        in_specs=(wide, wide, wide, deep, wide),
        out_specs=(wide, wide, wide, wide, deep),
        check_vma=False,
    )
```

```python
import functools

import jax
import jax.numpy as jnp
from jax import lax
from jax.experimental import pallas as pl
from jax.experimental.pallas import tpu as pltpu
from jax.sharding import PartitionSpec as P

F32 = jnp.float32
BF16 = jnp.bfloat16
EPS = 1e-06
VM = pl.BlockSpec(memory_space=pltpu.VMEM)
HB = pl.BlockSpec(memory_space=pltpu.HBM)


def mm(a, b):
    return lax.dot_general(a, b, (((1,), (0,)), ((), ())), preferred_element_type=F32)


def mm_rt(a, b):
    return lax.dot_general(a, b, (((1,), (1,)), ((), ())), preferred_element_type=F32)


def mm_lt(a, b):
    return lax.dot_general(a, b, (((0,), (0,)), ((), ())), preferred_element_type=F32)


def causal(size):
    return lax.broadcasted_iota(jnp.int32, (size, size), 0) >= lax.broadcasted_iota(
        jnp.int32, (size, size), 1
    )


class Cut:
    def __init__(self, rows, heads, dim, group, groups):
        self.rows, self.heads, self.dim = rows, heads, dim
        self.per = heads // groups
        self.base = group * self.per
        self.size = 256 if rows % 256 == 0 else rows
        self.chunks = rows // self.size

    def rng(self, c):
        return slice(c * self.size, (c + 1) * self.size)

    def cols(self, h):
        return slice(h * self.dim, (h + 1) * self.dim)

    def whole(self, h):
        return self.cols(self.base + h)

    def each(self):
        return [(h, c) for h in range(self.per) for c in range(self.chunks)]

    def span(self):
        return pl.ds(self.base * self.dim, self.per * self.dim)


def state_kernel(cut, k_hbm, v_hbm, q_hbm, total_ref, before_ref, k_ref, v_ref, q_ref, sems, q_sem):
    width = 2 * cut.dim
    pieces = k_ref.shape[1] // width

    def copy(i, j):
        src, dst = ((k_hbm, k_ref), (v_hbm, v_ref))[j]
        at = pl.ds(i * width, width)
        return pltpu.make_async_copy(src.at[:, at], dst.at[:, at], sems.at[j, i])

    for i in range(pieces):
        copy(i, 0).start()
        copy(i, 1).start()
    last = pltpu.make_async_copy(q_hbm, q_ref, q_sem)
    last.start()
    for h in range(cut.per):
        if h % 2 == 0:
            copy(h // 2, 0).wait()
            copy(h // 2, 1).wait()
        terms = [
            mm_lt(k_ref[cut.rng(c), cut.whole(h)], v_ref[cut.rng(c), cut.whole(h)])
            for c in range(cut.chunks)
        ]
        run = jnp.zeros((cut.dim, cut.dim), F32)
        for c in range(cut.chunks):
            before_ref[h, c] = run
            run = run + terms[c]
        total_ref[h] = run
    last.wait()


def inner_kernel(
    cut, q_ref, k_ref, v_ref, before_ref, side_hbm, att_ref, scores_ref, side_ref, side_sem
):
    side = pltpu.make_async_copy(side_hbm, side_ref, side_sem)
    side.start()
    keep = causal(cut.size)
    each = cut.each()
    q = {j: q_ref[cut.rng(j[1]), cut.whole(j[0])] for j in each}
    k = {j: k_ref[cut.rng(j[1]), cut.whole(j[0])] for j in each}
    v = {j: v_ref[cut.rng(j[1]), cut.whole(j[0])] for j in each}
    scores = {j: jnp.where(keep, mm_rt(q[j], k[j]), 0.0).astype(BF16) for j in each}
    att = {j: mm(scores[j], v[j]) for j in each}
    for h, c in each:
        if c > 0:
            before = before_ref[cut.base + h, c].astype(BF16)
            att[h, c] = att[h, c] + mm(q[h, c], before)
    for h, c in each:
        scores_ref[h, c] = scores[h, c]
        att_ref[cut.rng(c), cut.cols(h)] = att[h, c]
    side.wait()


def far_of(per, h, own_half, other_half):
    half = per // 2
    first = lax.rem(lax.axis_index("ctx"), 2) == 0
    mine, other = own_half[h % half], other_half[h % half]
    return jnp.where(first == (h < half), mine, other)


def norm_kernel(cut, masked, *refs):
    att_ref, q_ref, g_ref, init_ref, near_ref, far_ref, other_ref = refs[:7]
    out_hbm, ga_ref, total_ref, after_ref, prefix_ref, out_ref, sems = refs[-7:]
    place = lax.axis_index("ctx")
    add_near = lax.rem(place, 2) == 1
    add_far = place >= 2
    copies = []
    for h in range(cut.per):
        full = far_of(cut.per, h, far_ref, other_ref)
        if not masked:
            full = jnp.where(add_far, full, 0.0)
        prefix_ref[h] = init_ref[cut.base + h] + (full + jnp.where(add_near, near_ref[cut.base + h], 0.0))
    ga = {}
    for h, c in cut.each():
        q = q_ref[cut.rng(c), cut.whole(h)]
        att = att_ref[cut.rng(c), cut.cols(h)] + mm(q, prefix_ref[h].astype(BF16))
        up = g_ref[cut.rng(c), cut.whole(h)].astype(F32)
        square = jnp.sum(att * att, axis=-1, keepdims=True)
        along = jnp.sum(up * att, axis=-1, keepdims=True)
        inv = lax.rsqrt(square * (1.0 / cut.dim) + EPS)
        normed = att * inv
        ga[h, c] = (inv * (up - normed * (along * (inv * (1.0 / cut.dim))))).astype(BF16)
        out_ref[cut.rng(c), cut.cols(h)] = normed.astype(BF16)
        ga_ref[cut.rng(c), cut.cols(h)] = ga[h, c]
        if h % 2 == 1 and c == cut.chunks - 1:
            i = h // 2
            copies.append(
                pltpu.make_async_copy(
                    out_ref.at[:, pl.ds(2 * i * cut.dim, 2 * cut.dim)],
                    out_hbm.at[:, pl.ds((cut.base + 2 * i) * cut.dim, 2 * cut.dim)],
                    sems.at[i],
                )
            )
            copies[-1].start()
    terms = {(h, c): mm_lt(q_ref[cut.rng(c), cut.whole(h)], ga[h, c]) for h, c in cut.each()}
    for h in range(cut.per):
        run = jnp.zeros((cut.dim, cut.dim), F32)
        for c in reversed(range(cut.chunks)):
            after_ref[h, c] = run
            run = run + terms[h, c]
        total_ref[h] = run
    for copy in copies:
        copy.wait()


def back_kernel(cut, *refs):
    q_ref, k_ref, v_ref, ga_ref, prefix_ref, before_ref, scores_ref = refs[:7]
    qg_hbm, kg_ref, vg_ref, qg_ref, sems = refs[-5:]
    keep = causal(cut.size)
    each = cut.each()
    q = {j: q_ref[cut.rng(j[1]), cut.whole(j[0])] for j in each}
    k = {j: k_ref[cut.rng(j[1]), cut.whole(j[0])] for j in each}
    v = {j: v_ref[cut.rng(j[1]), cut.whole(j[0])] for j in each}
    ga = {j: ga_ref[cut.rng(j[1]), cut.cols(j[0])] for j in each}
    state = {(h, c): (prefix_ref[h] + before_ref[cut.base + h, c]).astype(BF16) for h, c in each}
    scores = {j: scores_ref[j[0], j[1]] for j in each}
    grad = {j: jnp.where(keep, mm_rt(ga[j], v[j]), 0.0).astype(BF16) for j in each}
    qg = {j: mm(grad[j], k[j]) + mm_rt(ga[j], state[j]) for j in each}
    for h, c in each:
        qg_ref[cut.rng(c), cut.cols(h)] = qg[h, c].astype(BF16)
    copies = []
    for i in range(cut.per // 2):
        copies.append(
            pltpu.make_async_copy(
                qg_ref.at[:, pl.ds(2 * i * cut.dim, 2 * cut.dim)],
                qg_hbm.at[:, pl.ds((cut.base + 2 * i) * cut.dim, 2 * cut.dim)],
                sems.at[i],
            )
        )
        copies[-1].start()
    vg = {j: mm_lt(scores[j], ga[j]) for j in each}
    kg = {j: mm_lt(grad[j], q[j]) for j in each}
    for h, c in each:
        kg_ref[cut.rng(c), cut.cols(h)] = kg[h, c]
        vg_ref[cut.rng(c), cut.cols(h)] = vg[h, c]
    for copy in copies:
        copy.wait()


def last_kernel(cut, masked, *refs):
    k_ref, v_ref, kp_ref, vp_ref, after_ref, own_ref, near_ref = refs[:7]
    far_ref, other_ref, all_ref, all_other_ref = refs[7:11]
    kg_hbm, vg_hbm, sg_hbm, kg_ref, vg_ref, sg_ref, sems, sg_sem = refs[-8:]
    place = lax.axis_index("ctx")
    add_near = lax.rem(place, 2) == 0
    add_far = place < 2
    copies = []
    for h in range(cut.per):
        near = near_ref[h]
        full = far_of(cut.per, h, far_ref, other_ref)
        every = far_of(cut.per, h, all_ref, all_other_ref)
        sg_ref[h] = every + (own_ref[h] + near)
        if not masked:
            full = jnp.where(add_far, full, 0.0)
        suffix = full + jnp.where(add_near, near, 0.0)
        cols, whole = cut.cols(h), cut.whole(h)
        for c in range(cut.chunks):
            rows = cut.rng(c)
            state = (suffix + after_ref[h, c]).astype(BF16)
            kg_ref[rows, cols] = (kp_ref[rows, cols] + mm_rt(v_ref[rows, whole], state)).astype(BF16)
            vg_ref[rows, cols] = (vp_ref[rows, cols] + mm(k_ref[rows, whole], state)).astype(BF16)
        if h % 2 == 1:
            i = h // 2
            for j, (src, dst) in enumerate(((kg_ref, kg_hbm), (vg_ref, vg_hbm))):
                copies.append(
                    pltpu.make_async_copy(
                        src.at[:, pl.ds(2 * i * cut.dim, 2 * cut.dim)],
                        dst.at[:, pl.ds((cut.base + 2 * i) * cut.dim, 2 * cut.dim)],
                        sems.at[j, i],
                    )
                )
                copies[-1].start()
    copies.append(
        pltpu.make_async_copy(sg_ref, sg_hbm.at[pl.ds(cut.base, cut.per)], sg_sem)
    )
    copies[-1].start()
    for copy in copies:
        copy.wait()


def half_kernel(per, own_ref, near_ref, *mine_refs):
    half = per // 2
    first = lax.rem(lax.axis_index("ctx"), 2) == 0
    for g, mine_ref in enumerate(mine_refs):
        for h in range(half):
            low, high = g * per + h, g * per + half + h
            mine_ref[h] = jnp.where(
                first, own_ref[low] + near_ref[low], own_ref[high] + near_ref[high]
            )


def shards(n, groups, queries, keys, values, init_state, out_grad):
    rows, width = queries.shape
    heads, dim = init_state.shape[:2]
    pairs = n // 2
    swap_pairs = [(i, i ^ 1) for i in range(n)]
    shift_pairs = [(i, (i + 2) % n) for i in range(n)]
    swap = lambda x: lax.ppermute(x, "ctx", swap_pairs)
    shift = lambda x: lax.ppermute(x, "ctx", shift_pairs)
    cuts = [Cut(rows, heads, dim, g, groups) for g in range(groups)]
    per, chunks, size = cuts[0].per, cuts[0].chunks, cuts[0].size
    wide_b = jax.ShapeDtypeStruct((rows, width), BF16)
    all_b = pltpu.VMEM((rows, width), BF16)
    part_b = pltpu.VMEM((rows, per * dim), BF16)
    part_f = pltpu.VMEM((rows, per * dim), F32)
    state_f = pltpu.VMEM((per, dim, dim), F32)
    states_f = pltpu.VMEM((per, chunks, dim, dim), F32)
    scores_b = pltpu.VMEM((per, chunks, size, size), BF16)
    small = 2 * per * rows * dim * dim
    square = 2 * per * rows * size * dim
    piece = rows * per * dim * 2
    dma = pltpu.SemaphoreType.DMA

    def call(body, name, ins, outs, scratch, flops, nbytes, kept=()):
        ins = list(ins)
        aliases = {len(ins) + i: i for i in range(len(kept))}
        specs = [VM] * len(ins) + [HB] * len(kept)
        out_specs = [VM if isinstance(o, type(all_b)) else HB for o in outs]
        return pl.pallas_call(
            body,
            in_specs=specs,
            out_specs=out_specs,
            out_shape=list(outs),
            scratch_shapes=scratch,
            input_output_aliases=aliases,
            compiler_params=pltpu.CompilerParams(vmem_limit_bytes=16 * 1024 * 1024),
            cost_estimate=pl.CostEstimate(flops=flops, bytes_accessed=nbytes, transcendentals=0),
            name=name,
        )(*ins, *kept)

    def far_sums(mine, later):
        if pairs == 2:
            far = shift(mine)
            return far, far
        pair = lax.axis_index("ctx") // 2
        moving = mine
        used, every = jnp.zeros_like(mine), jnp.zeros_like(mine)
        for j in range(1, pairs):
            moving = shift(moving)
            wrapped = pair < j
            used = used + jnp.where(wrapped == later, moving, 0.0)
            every = every + moving
        return used, every

    def halves(own, near, count):
        return pl.pallas_call(
            functools.partial(half_kernel, per),
            in_specs=[VM] * 2,
            out_specs=[VM] * count,
            out_shape=[pltpu.VMEM((per // 2, dim, dim), F32)] * count,
            compiler_params=pltpu.CompilerParams(vmem_limit_bytes=4 * 1024 * 1024),
            name="half",
        )(own, near)

    masked = pairs != 2

    def call_inner(g, side):
        return pl.pallas_call(
            functools.partial(inner_kernel, cuts[g]),
            in_specs=[VM] * 4 + [HB],
            out_specs=[VM] * 3,
            out_shape=[part_f, scores_b, pltpu.VMEM(side.shape, side.dtype)],
            scratch_shapes=[dma],
            compiler_params=pltpu.CompilerParams(vmem_limit_bytes=16 * 1024 * 1024),
            cost_estimate=pl.CostEstimate(
                flops=2 * square + small, bytes_accessed=piece, transcendentals=0
            ),
            name="inner%d" % g,
        )(queries_v, keys_v, values_v, before, in_hbm(side))

    in_hbm = lambda x: pltpu.with_memory_space_constraint(x, pltpu.HBM)
    every = Cut(rows, heads, dim, 0, 1)
    own, before, keys_v, values_v, queries_v = pl.pallas_call(
        functools.partial(state_kernel, every),
        in_specs=[HB] * 3,
        out_specs=[VM] * 5,
        out_shape=[
            pltpu.VMEM((heads, dim, dim), F32),
            pltpu.VMEM((heads, chunks, dim, dim), F32),
            all_b,
            all_b,
            all_b,
        ],
        scratch_shapes=[dma((2, heads // 2)), dma],
        compiler_params=pltpu.CompilerParams(vmem_limit_bytes=16 * 1024 * 1024),
        cost_estimate=pl.CostEstimate(
            flops=2 * small, bytes_accessed=6 * piece, transcendentals=0
        ),
        name="states",
    )(in_hbm(keys), in_hbm(values), in_hbm(queries))
    att, scores, far, other = {}, {}, {}, {}
    near = swap(own)
    att[0], scores[0], out_grad_v = call_inner(0, out_grad)
    near, att[0] = lax.optimization_barrier((near, att[0]))
    mine = halves(own, near, groups)
    for g in range(groups):
        far[g], _ = far_sums(mine[g], False)
    att[1], scores[1], init_v = call_inner(1, init_state)
    far[0], att[1] = lax.optimization_barrier((far[0], att[1]))
    for g in range(groups):
        other[g] = swap(far[g])
    ga, total, after, prefix = {}, {}, {}, {}
    output = ()
    gnear, gfar, gall = {}, {}, {}
    for g, cut in enumerate(cuts):
        out, ga[g], total[g], after[g], prefix[g] = call(
            functools.partial(norm_kernel, cut, masked),
            "norm%d" % g,
            [att[g], queries_v, out_grad_v, init_v, near, far[g], other[g]],
            [wide_b, part_b, state_f, states_f, state_f],
            [pltpu.VMEM((rows, per * dim), BF16), dma((per // 2,))],
            2 * small,
            piece,
            output,
        )
        output = (out,)
        gnear[g] = swap(total[g])
    gnear[0], total[1] = lax.optimization_barrier((gnear[0], total[1]))
    for g, cut in enumerate(cuts):
        gfar[g], gall[g] = far_sums(halves(total[g], gnear[g], 1)[0], True)
    kp, vp = {}, {}
    query_grad = ()
    for g, cut in enumerate(cuts):
        out, kp[g], vp[g] = call(
            functools.partial(back_kernel, cut),
            "back%d" % g,
            [queries_v, keys_v, values_v, ga[g], prefix[g], before, scores[g]],
            [wide_b, part_f, part_f],
            [pltpu.VMEM((rows, per * dim), BF16), dma((per // 2,))],
            4 * square + small,
            piece,
            query_grad,
        )
        query_grad = (out,)
        gfar[g], gall[g], kp[g] = lax.optimization_barrier((gfar[g], gall[g], kp[g]))
    ends = ()
    for g, cut in enumerate(cuts):
        used = swap(gfar[g])
        total_far = used if pairs == 2 else swap(gall[g])
        ends = call(
            functools.partial(last_kernel, cut, masked),
            "last%d" % g,
            [
                keys_v, values_v, kp[g], vp[g], after[g], total[g], gnear[g],
                gfar[g], used, gall[g], total_far,
            ],
            [wide_b, wide_b, jax.ShapeDtypeStruct(init_state.shape, F32)],
            [
                pltpu.VMEM((rows, per * dim), BF16),
                pltpu.VMEM((rows, per * dim), BF16),
                pltpu.VMEM((per, dim, dim), F32),
                dma((2, per // 2)),
                dma,
            ],
            2 * small,
            2 * piece,
            ends,
        )
    key_grad, value_grad, state_grad = ends
    return output[0], query_grad[0], key_grad, value_grad, state_grad


def solution(mesh):
    wide = P(("grp", "ctx"), "head")
    deep = P(("grp", "head"), None, None)
    return jax.shard_map(
        functools.partial(shards, mesh.shape["ctx"], 2),
        mesh=mesh,
        in_specs=(wide, wide, wide, deep, wide),
        out_specs=(wide, wide, wide, wide, deep),
        check_vma=False,
    )
```

```python
import functools

import jax
import jax.numpy as jnp
from jax import lax
from jax.experimental import pallas as pl
from jax.experimental.pallas import tpu as pltpu
from jax.sharding import PartitionSpec as P

F32 = jnp.float32
BF16 = jnp.bfloat16
EPS = 1e-06
VM = pl.BlockSpec(memory_space=pltpu.VMEM)
HB = pl.BlockSpec(memory_space=pltpu.HBM)


def mm(a, b):
    return lax.dot_general(a, b, (((1,), (0,)), ((), ())), preferred_element_type=F32)


def mm_rt(a, b):
    return lax.dot_general(a, b, (((1,), (1,)), ((), ())), preferred_element_type=F32)


def mm_lt(a, b):
    return lax.dot_general(a, b, (((0,), (0,)), ((), ())), preferred_element_type=F32)


def causal(size):
    return lax.broadcasted_iota(jnp.int32, (size, size), 0) >= lax.broadcasted_iota(
        jnp.int32, (size, size), 1
    )


class Cut:
    def __init__(self, rows, heads, dim, group, groups):
        self.rows, self.heads, self.dim = rows, heads, dim
        self.per = heads // groups
        self.base = group * self.per
        self.size = 256 if rows % 256 == 0 else rows
        self.chunks = rows // self.size

    def rng(self, c):
        return slice(c * self.size, (c + 1) * self.size)

    def cols(self, h):
        return slice(h * self.dim, (h + 1) * self.dim)

    def whole(self, h):
        return self.cols(self.base + h)

    def each(self):
        return [(h, c) for h in range(self.per) for c in range(self.chunks)]

    def span(self):
        return pl.ds(self.base * self.dim, self.per * self.dim)


def column_copies(pairs, sems):
    copies = [pltpu.make_async_copy(src, dst, sems.at[i]) for i, (src, dst) in enumerate(pairs)]
    for copy in copies:
        copy.start()
    return copies


def state_kernel(cut, k_hbm, v_hbm, _, total_ref, before_ref, k_ref, v_ref, sems):
    width = 2 * cut.dim

    def copy(i, j):
        src, dst = ((k_hbm, k_ref), (v_hbm, v_ref))[j]
        from_at = pl.ds(cut.base * cut.dim + i * width, width)
        return pltpu.make_async_copy(
            src.at[:, from_at], dst.at[:, pl.ds(i * width, width)], sems.at[j, i]
        )

    for i in range(cut.per // 2):
        copy(i, 0).start()
        copy(i, 1).start()
    for h in range(cut.per):
        if h % 2 == 0:
            copy(h // 2, 0).wait()
            copy(h // 2, 1).wait()
        terms = [
            mm_lt(k_ref[cut.rng(c), cut.cols(h)], v_ref[cut.rng(c), cut.cols(h)])
            for c in range(cut.chunks)
        ]
        run = jnp.zeros((cut.dim, cut.dim), F32)
        for c in range(cut.chunks):
            before_ref[h, c] = run
            run = run + terms[c]
        total_ref[h] = run


def inner_kernel(cut, q_ref, k_ref, v_ref, before_ref, att_ref, scores_ref):
    keep = causal(cut.size)
    each = cut.each()
    q = {(h, c): q_ref[cut.rng(c), cut.whole(h)] for h, c in each}
    k = {(h, c): k_ref[cut.rng(c), cut.cols(h)] for h, c in each}
    v = {(h, c): v_ref[cut.rng(c), cut.cols(h)] for h, c in each}
    scores = {j: jnp.where(keep, mm_rt(q[j], k[j]), 0.0).astype(BF16) for j in each}
    att = {j: mm(scores[j], v[j]) for j in each}
    for h, c in each:
        if c > 0:
            att[h, c] = att[h, c] + mm(q[h, c], before_ref[h, c].astype(BF16))
    for h, c in each:
        scores_ref[h, c] = scores[h, c]
        att_ref[cut.rng(c), cut.cols(h)] = att[h, c]


def far_of(per, h, own_half, other_half):
    half = per // 2
    first = lax.rem(lax.axis_index("ctx"), 2) == 0
    mine, other = own_half[h % half], other_half[h % half]
    return jnp.where(first == (h < half), mine, other)


def norm_kernel(cut, masked, *refs):
    att_ref, q_ref, g_ref, init_ref, near_ref, far_ref, other_ref = refs[:7]
    out_ref, ga_ref, total_ref, after_ref, prefix_ref = refs[7:]
    place = lax.axis_index("ctx")
    add_near = lax.rem(place, 2) == 1
    add_far = place >= 2
    for h in range(cut.per):
        full = far_of(cut.per, h, far_ref, other_ref)
        if not masked:
            full = jnp.where(add_far, full, 0.0)
        prefix_ref[h] = init_ref[cut.base + h] + (full + jnp.where(add_near, near_ref[h], 0.0))
    ga = {}
    for h, c in cut.each():
        q = q_ref[cut.rng(c), cut.whole(h)]
        att = att_ref[cut.rng(c), cut.cols(h)] + mm(q, prefix_ref[h].astype(BF16))
        up = g_ref[cut.rng(c), cut.whole(h)].astype(F32)
        square = jnp.sum(att * att, axis=-1, keepdims=True)
        along = jnp.sum(up * att, axis=-1, keepdims=True)
        inv = lax.rsqrt(square * (1.0 / cut.dim) + EPS)
        normed = att * inv
        ga[h, c] = (inv * (up - normed * (along * (inv * (1.0 / cut.dim))))).astype(BF16)
        out_ref[cut.rng(c), cut.cols(h)] = normed.astype(BF16)
        ga_ref[cut.rng(c), cut.cols(h)] = ga[h, c]
    terms = {(h, c): mm_lt(q_ref[cut.rng(c), cut.whole(h)], ga[h, c]) for h, c in cut.each()}
    for h in range(cut.per):
        run = jnp.zeros((cut.dim, cut.dim), F32)
        for c in reversed(range(cut.chunks)):
            after_ref[h, c] = run
            run = run + terms[h, c]
        total_ref[h] = run


def back_kernel(cuts, g, *refs):
    cut = cuts[g]
    count = len(cuts) if g == 0 else 0
    q_ref, k_ref, v_ref, ga_ref, prefix_ref, before_ref, scores_ref = refs[:7]
    ready = refs[7 : 7 + count]
    qg_ref, kg_ref, vg_ref = refs[7 + count : 10 + count]
    copies = []
    if g == 0:
        hbm, sems = refs[10 + count :]
        copies = column_copies([(r, hbm.at[:, cuts[i].span()]) for i, r in enumerate(ready)], sems)
    keep = causal(cut.size)
    each = cut.each()
    q = {j: q_ref[cut.rng(j[1]), cut.whole(j[0])] for j in each}
    k = {j: k_ref[cut.rng(j[1]), cut.cols(j[0])] for j in each}
    v = {j: v_ref[cut.rng(j[1]), cut.cols(j[0])] for j in each}
    ga = {j: ga_ref[cut.rng(j[1]), cut.cols(j[0])] for j in each}
    state = {
        (h, c): (prefix_ref[h] + before_ref[h, c]).astype(BF16) for h, c in each
    }
    scores = {j: scores_ref[j[0], j[1]] for j in each}
    grad = {j: jnp.where(keep, mm_rt(ga[j], v[j]), 0.0).astype(BF16) for j in each}
    qg = {j: mm(grad[j], k[j]) + mm_rt(ga[j], state[j]) for j in each}
    for h, c in each:
        qg_ref[cut.rng(c), cut.cols(h)] = qg[h, c].astype(BF16)
    vg = {j: mm(ga[j].T, scores[j]) for j in each}
    kg = {j: mm(q[j].T, grad[j]) for j in each}
    for h, c in each:
        kg_ref[cut.cols(h), cut.rng(c)] = kg[h, c]
        vg_ref[cut.cols(h), cut.rng(c)] = vg[h, c]
    for copy in copies:
        copy.wait()


def last_kernel(cuts, g, masked, *refs):
    cut = cuts[g]
    k_ref, v_ref, kp_ref, vp_ref, after_ref, own_ref, near_ref = refs[:7]
    far_ref, other_ref, all_ref, all_other_ref = refs[7:11]
    final = g == len(cuts) - 1
    if g == 0:
        grads, refs = refs[11 : 11 + len(cuts)], refs[11 + len(cuts) :]
    else:
        ready, refs = [refs[11 + 3 * i : 14 + 3 * i] for i in range(g)], refs[11 + 3 * g :]
    if final:
        kg_hbm, vg_hbm, sg_hbm, kg_ref, vg_ref, sg_ref, ready_sems, sems, sg_sem = refs
    else:
        kg_ref, vg_ref, sg_ref = refs[:3]
    place = lax.axis_index("ctx")
    add_near = lax.rem(place, 2) == 0
    add_far = place < 2
    copies = []
    if g == 0:
        hbm, qg_sems = refs[3:]
        copies += column_copies(
            [(r, hbm.at[:, cuts[i].span()]) for i, r in enumerate(grads)], qg_sems
        )
    if final:
        pairs = []
        for i, (kg, vg, sg) in enumerate(ready):
            at = cuts[i].span()
            pairs += [(kg, kg_hbm.at[:, at]), (vg, vg_hbm.at[:, at])]
            pairs += [(sg, sg_hbm.at[pl.ds(cuts[i].base, cut.per)])]
        copies += column_copies(pairs, ready_sems)
    for h in range(cut.per):
        near = near_ref[h]
        full = far_of(cut.per, h, far_ref, other_ref)
        every = far_of(cut.per, h, all_ref, all_other_ref)
        sg_ref[h] = every + (own_ref[h] + near)
        if not masked:
            full = jnp.where(add_far, full, 0.0)
        suffix = full + jnp.where(add_near, near, 0.0)
        cols = cut.cols(h)
        for c in range(cut.chunks):
            rows = cut.rng(c)
            state = (suffix + after_ref[h, c]).astype(BF16)
            kg = kp_ref[cols, rows] + mm_rt(state, v_ref[rows, cols])
            vg = vp_ref[cols, rows] + mm_rt(state.T, k_ref[rows, cols])
            kg_ref[rows, cols] = kg.astype(BF16).T
            vg_ref[rows, cols] = vg.astype(BF16).T
        if final:
            at, to = pl.ds(h * cut.dim, cut.dim), pl.ds((cut.base + h) * cut.dim, cut.dim)
            copies += column_copies(
                [(kg_ref.at[:, at], kg_hbm.at[:, to]), (vg_ref.at[:, at], vg_hbm.at[:, to])],
                sems.at[h],
            )
    if final:
        copies += column_copies([(sg_ref, sg_hbm.at[pl.ds(cut.base, cut.per)])], sg_sem)
    for copy in copies:
        copy.wait()


def half_kernel(own_ref, near_ref, mine_ref):
    half = mine_ref.shape[0]
    first = lax.rem(lax.axis_index("ctx"), 2) == 0
    for h in range(half):
        mine_ref[h] = jnp.where(
            first, own_ref[h] + near_ref[h], own_ref[half + h] + near_ref[half + h]
        )


def shards(n, groups, queries, keys, values, init_state, out_grad):
    rows, width = queries.shape
    heads, dim = init_state.shape[:2]
    pairs = n // 2
    swap_pairs = [(i, i ^ 1) for i in range(n)]
    shift_pairs = [(i, (i + 2) % n) for i in range(n)]
    swap = lambda x: lax.ppermute(x, "ctx", swap_pairs)
    shift = lambda x: lax.ppermute(x, "ctx", shift_pairs)
    cuts = [Cut(rows, heads, dim, g, groups) for g in range(groups)]
    per, chunks, size = cuts[0].per, cuts[0].chunks, cuts[0].size
    wide_b = jax.ShapeDtypeStruct((rows, width), BF16)
    all_b = pltpu.VMEM((rows, width), BF16)
    part_b = pltpu.VMEM((rows, per * dim), BF16)
    part_f = pltpu.VMEM((rows, per * dim), F32)
    part_ft = pltpu.VMEM((per * dim, rows), F32)
    state_f = pltpu.VMEM((per, dim, dim), F32)
    states_f = pltpu.VMEM((per, chunks, dim, dim), F32)
    scores_b = pltpu.VMEM((per, chunks, size, size), BF16)
    small = 2 * per * rows * dim * dim
    square = 2 * per * rows * size * dim
    piece = rows * per * dim * 2
    dma = pltpu.SemaphoreType.DMA

    def call(body, name, ins, outs, scratch, flops, nbytes):
        return pl.pallas_call(
            body,
            in_specs=[VM] * len(ins),
            out_specs=[HB if isinstance(o, jax.ShapeDtypeStruct) else VM for o in outs],
            out_shape=list(outs),
            scratch_shapes=scratch,
            compiler_params=pltpu.CompilerParams(vmem_limit_bytes=16 * 1024 * 1024),
            cost_estimate=pl.CostEstimate(flops=flops, bytes_accessed=nbytes, transcendentals=0),
            name=name,
        )(*ins)

    def far_sums(mine, later):
        if pairs == 2:
            far = shift(mine)
            return far, far
        pair = lax.axis_index("ctx") // 2
        moving = mine
        used, every = jnp.zeros_like(mine), jnp.zeros_like(mine)
        for j in range(1, pairs):
            moving = shift(moving)
            wrapped = pair < j
            used = used + jnp.where(wrapped == later, moving, 0.0)
            every = every + moving
        return used, every

    def half_of(own, near):
        return pl.pallas_call(
            half_kernel,
            in_specs=[VM] * 2,
            out_specs=VM,
            out_shape=pltpu.VMEM((per // 2, dim, dim), F32),
            compiler_params=pltpu.CompilerParams(vmem_limit_bytes=4 * 1024 * 1024),
            name="half",
        )(own, near)

    masked = pairs != 2

    def state_call(g):
        order = keys if g == 0 else own[g - 1]
        return pl.pallas_call(
            functools.partial(state_kernel, cuts[g]),
            in_specs=[HB, HB, HB if g == 0 else VM],
            out_specs=[VM] * 4,
            out_shape=[state_f, states_f, part_b, part_b],
            scratch_shapes=[dma((2, per // 2))],
            compiler_params=pltpu.CompilerParams(vmem_limit_bytes=16 * 1024 * 1024),
            cost_estimate=pl.CostEstimate(
                flops=small, bytes_accessed=2 * piece, transcendentals=0
            ),
            name="states%d" % g,
        )(in_hbm(keys), in_hbm(values), in_hbm(order) if g == 0 else order)

    in_hbm = lambda x: pltpu.with_memory_space_constraint(x, pltpu.HBM)
    own, before, near, keys_v, values_v = {}, {}, {}, {}, {}
    for g, cut in enumerate(cuts):
        own[g], before[g], keys_v[g], values_v[g] = state_call(g)
        near[g] = swap(own[g])
    att, scores, far, other = {}, {}, {}, {}
    for g in range(groups):
        mine = half_of(own[g], near[g])
        far[g], _ = far_sums(mine, False)
        if g == groups - 1:
            mine, before[0] = lax.optimization_barrier((mine, before[0]))
    for g, cut in enumerate(cuts):
        att[g], scores[g] = call(
            functools.partial(inner_kernel, cut),
            "inner%d" % g,
            [queries, keys_v[g], values_v[g], before[g]],
            [part_f, scores_b],
            [],
            2 * square + small,
            0,
        )
    far[0], att[0], att[1] = lax.optimization_barrier((far[0], att[0], att[1]))
    for g in range(groups):
        other[g] = swap(far[g])
    out, ga, total, after, prefix = {}, {}, {}, {}, {}
    gnear, gfar, gall = {}, {}, {}
    for g, cut in enumerate(cuts):
        out[g], ga[g], total[g], after[g], prefix[g] = call(
            functools.partial(norm_kernel, cut, masked),
            "norm%d" % g,
            [att[g], queries, out_grad, init_state, near[g], far[g], other[g]],
            [part_b, part_b, state_f, states_f, state_f],
            [],
            2 * small,
            piece,
        )
        gnear[g] = swap(total[g])
    gnear[0], total[1] = lax.optimization_barrier((gnear[0], total[1]))
    for g, cut in enumerate(cuts):
        gfar[g], gall[g] = far_sums(half_of(total[g], gnear[g]), True)
    kp, vp, qg = {}, {}, {}
    for g, cut in enumerate(cuts):
        ready = list(out.values()) if g == 0 else []
        qg[g], kp[g], vp[g], *written = call(
            functools.partial(back_kernel, cuts, g),
            "back%d" % g,
            [queries, keys_v[g], values_v[g], ga[g], prefix[g], before[g], scores[g], *ready],
            [part_b, part_ft, part_ft] + [wide_b] * (g == 0),
            [dma((groups,))] if g == 0 else [],
            4 * square + small,
            piece,
        )
        if g == 0:
            (output,) = written
        gfar[g], gall[g], kp[g] = lax.optimization_barrier((gfar[g], gall[g], kp[g]))
    ready = list(qg.values())
    for g, cut in enumerate(cuts):
        used = swap(gfar[g])
        total_far = used if pairs == 2 else swap(gall[g])
        ins = [
            keys_v[g], values_v[g], kp[g], vp[g], after[g], total[g], gnear[g],
            gfar[g], used, gall[g], total_far,
        ]
        outs, scratch = [part_b, part_b, state_f], []
        if g == groups - 1:
            scratch = outs + [dma((3 * g,)), dma((per, 2)), dma((1,))]
            outs = [wide_b, wide_b, jax.ShapeDtypeStruct(init_state.shape, F32)]
        elif g == 0:
            outs, scratch = outs + [wide_b], [dma((groups,))]
        ends = list(
            call(
                functools.partial(last_kernel, cuts, g, masked),
                "last%d" % g,
                ins + ready,
                outs,
                scratch,
                2 * small,
                2 * piece,
            )
        )
        if g == 0:
            ready, query_grad = [], ends.pop()
        ready += ends
    key_grad, value_grad, state_grad = ends
    return output, query_grad, key_grad, value_grad, state_grad


def solution(mesh):
    wide = P(("grp", "ctx"), "head")
    deep = P(("grp", "head"), None, None)
    return jax.shard_map(
        functools.partial(shards, mesh.shape["ctx"], 2),
        mesh=mesh,
        in_specs=(wide, wide, wide, deep, wide),
        out_specs=(wide, wide, wide, wide, deep),
        check_vma=False,
    )
```

```python
import functools

import jax
import jax.numpy as jnp
from jax import lax
from jax.experimental import pallas as pl
from jax.experimental.pallas import tpu as pltpu
from jax.sharding import PartitionSpec as P

F32 = jnp.float32
BF16 = jnp.bfloat16
EPS = 1e-06
VM = pl.BlockSpec(memory_space=pltpu.VMEM)
HB = pl.BlockSpec(memory_space=pltpu.HBM)


def mm(a, b):
    return lax.dot_general(a, b, (((1,), (0,)), ((), ())), preferred_element_type=F32)


def mm_rt(a, b):
    return lax.dot_general(a, b, (((1,), (1,)), ((), ())), preferred_element_type=F32)


def mm_lt(a, b):
    return lax.dot_general(a, b, (((0,), (0,)), ((), ())), preferred_element_type=F32)


def causal(size):
    return lax.broadcasted_iota(jnp.int32, (size, size), 0) >= lax.broadcasted_iota(
        jnp.int32, (size, size), 1
    )


class Cut:
    def __init__(self, rows, heads, dim, group, groups):
        self.rows, self.heads, self.dim = rows, heads, dim
        self.per = heads // groups
        self.base = group * self.per
        self.size = 256 if rows % 256 == 0 else rows
        self.chunks = rows // self.size

    def rng(self, c):
        return slice(c * self.size, (c + 1) * self.size)

    def cols(self, h):
        return slice(h * self.dim, (h + 1) * self.dim)

    def whole(self, h):
        return self.cols(self.base + h)

    def each(self):
        return [(h, c) for h in range(self.per) for c in range(self.chunks)]

    def span(self):
        return pl.ds(self.base * self.dim, self.per * self.dim)


def column_copies(pairs, sems):
    copies = [pltpu.make_async_copy(src, dst, sems.at[i]) for i, (src, dst) in enumerate(pairs)]
    for copy in copies:
        copy.start()
    return copies


def state_kernel(cut, k_hbm, v_hbm, _, total_ref, before_ref, k_ref, v_ref, sems):
    width = 2 * cut.dim

    def copy(i, j):
        src, dst = ((k_hbm, k_ref), (v_hbm, v_ref))[j]
        from_at = pl.ds(cut.base * cut.dim + i * width, width)
        return pltpu.make_async_copy(
            src.at[:, from_at], dst.at[:, pl.ds(i * width, width)], sems.at[j, i]
        )

    for i in range(cut.per // 2):
        copy(i, 0).start()
        copy(i, 1).start()
    for h in range(cut.per):
        if h % 2 == 0:
            copy(h // 2, 0).wait()
            copy(h // 2, 1).wait()
        terms = [
            mm_lt(k_ref[cut.rng(c), cut.cols(h)], v_ref[cut.rng(c), cut.cols(h)])
            for c in range(cut.chunks)
        ]
        run = jnp.zeros((cut.dim, cut.dim), F32)
        for c in range(cut.chunks):
            before_ref[h, c] = run
            run = run + terms[c]
        total_ref[h] = run


def inner_kernel(cut, q_ref, k_ref, v_ref, before_ref, att_ref, scores_ref, qt_ref):
    keep = causal(cut.size)
    each = cut.each()
    q = {(h, c): q_ref[cut.rng(c), cut.whole(h)] for h, c in each}
    k = {(h, c): k_ref[cut.rng(c), cut.cols(h)] for h, c in each}
    v = {(h, c): v_ref[cut.rng(c), cut.cols(h)] for h, c in each}
    scores = {j: jnp.where(keep, mm_rt(q[j], k[j]), 0.0).astype(BF16) for j in each}
    att = {j: mm(scores[j], v[j]) for j in each}
    for h, c in each:
        if c > 0:
            att[h, c] = att[h, c] + mm(q[h, c], before_ref[h, c].astype(BF16))
    for h, c in each:
        scores_ref[h, c] = scores[h, c]
        att_ref[cut.rng(c), cut.cols(h)] = att[h, c]
        qt_ref[cut.cols(h), cut.rng(c)] = q[h, c].T


def far_of(per, h, own_half, other_half):
    half = per // 2
    first = lax.rem(lax.axis_index("ctx"), 2) == 0
    mine, other = own_half[h % half], other_half[h % half]
    return jnp.where(first == (h < half), mine, other)


def norm_kernel(cut, masked, *refs):
    att_ref, q_ref, qt_ref, g_ref, init_ref, near_ref, far_ref, other_ref = refs[:8]
    out_ref, ga_ref, total_ref, after_ref, prefix_ref = refs[8:]
    place = lax.axis_index("ctx")
    add_near = lax.rem(place, 2) == 1
    add_far = place >= 2
    for h in range(cut.per):
        full = far_of(cut.per, h, far_ref, other_ref)
        if not masked:
            full = jnp.where(add_far, full, 0.0)
        prefix_ref[h] = init_ref[cut.base + h] + (full + jnp.where(add_near, near_ref[h], 0.0))
    for h in range(cut.per):
        att = att_ref[:, cut.cols(h)] + mm(q_ref[:, cut.whole(h)], prefix_ref[h].astype(BF16))
        ga = []
        for c in range(cut.chunks):
            x = att[cut.rng(c)]
            up = g_ref[cut.rng(c), cut.whole(h)].astype(F32)
            square = jnp.sum(x * x, axis=-1, keepdims=True)
            along = jnp.sum(up * x, axis=-1, keepdims=True)
            inv = lax.rsqrt(square * (1.0 / cut.dim) + EPS)
            normed = x * inv
            ga.append((inv * (up - normed * (along * (inv * (1.0 / cut.dim))))).astype(BF16))
            out_ref[cut.rng(c), cut.cols(h)] = normed.astype(BF16)
            ga_ref[cut.rng(c), cut.cols(h)] = ga[c]
        run = jnp.zeros((cut.dim, cut.dim), F32)
        for c in reversed(range(cut.chunks)):
            after_ref[h, c] = run
            run = run + mm(qt_ref[cut.cols(h), cut.rng(c)], ga[c])
        total_ref[h] = run


def back_kernel(cuts, g, *refs):
    cut = cuts[g]
    count = len(cuts) if g == 0 else 0
    qt_ref, k_ref, v_ref, ga_ref, prefix_ref, before_ref, scores_ref = refs[:7]
    ready = refs[7 : 7 + count]
    qg_ref, kg_ref, vg_ref = refs[7 + count : 10 + count]
    copies = []
    if g == 0:
        hbm, sems = refs[10 + count :]
        copies = column_copies([(r, hbm.at[:, cuts[i].span()]) for i, r in enumerate(ready)], sems)
    keep = causal(cut.size)
    each = cut.each()
    qt = {j: qt_ref[cut.cols(j[0]), cut.rng(j[1])] for j in each}
    k = {j: k_ref[cut.rng(j[1]), cut.cols(j[0])] for j in each}
    v = {j: v_ref[cut.rng(j[1]), cut.cols(j[0])] for j in each}
    ga = {j: ga_ref[cut.rng(j[1]), cut.cols(j[0])] for j in each}
    state = {
        (h, c): (prefix_ref[h] + before_ref[h, c]).astype(BF16) for h, c in each
    }
    scores = {j: scores_ref[j[0], j[1]] for j in each}
    grad = {j: jnp.where(keep, mm_rt(ga[j], v[j]), 0.0).astype(BF16) for j in each}
    qg = {j: mm(grad[j], k[j]) + mm_rt(ga[j], state[j]) for j in each}
    for h, c in each:
        qg_ref[cut.rng(c), cut.cols(h)] = qg[h, c].astype(BF16)
    vg = {j: mm(ga[j].T, scores[j]) for j in each}
    kg = {j: mm(qt[j], grad[j]) for j in each}
    for h, c in each:
        kg_ref[cut.cols(h), cut.rng(c)] = kg[h, c]
        vg_ref[cut.cols(h), cut.rng(c)] = vg[h, c]
    for copy in copies:
        copy.wait()


def last_kernel(cuts, g, masked, *refs):
    cut = cuts[g]
    k_ref, v_ref, kp_ref, vp_ref, after_ref, own_ref, near_ref = refs[:7]
    far_ref, other_ref, all_ref, all_other_ref = refs[7:11]
    final = g == len(cuts) - 1
    if g == 0:
        grads, refs = refs[11 : 11 + len(cuts)], refs[11 + len(cuts) :]
    else:
        ready, refs = [refs[11 + 3 * i : 14 + 3 * i] for i in range(g)], refs[11 + 3 * g :]
    if final:
        kg_hbm, vg_hbm, sg_hbm, kg_ref, vg_ref, sg_ref, ready_sems, sems, sg_sem = refs
    else:
        kg_ref, vg_ref, sg_ref = refs[:3]
    place = lax.axis_index("ctx")
    add_near = lax.rem(place, 2) == 0
    add_far = place < 2
    copies = []
    if g == 0:
        hbm, qg_sems = refs[3:]
        copies += column_copies(
            [(r, hbm.at[:, cuts[i].span()]) for i, r in enumerate(grads)], qg_sems
        )
    if final:
        pairs = []
        for i, (kg, vg, sg) in enumerate(ready):
            at = cuts[i].span()
            pairs += [(kg, kg_hbm.at[:, at]), (vg, vg_hbm.at[:, at])]
            pairs += [(sg, sg_hbm.at[pl.ds(cuts[i].base, cut.per)])]
        copies += column_copies(pairs, ready_sems)
    for h in range(cut.per):
        near = near_ref[h]
        full = far_of(cut.per, h, far_ref, other_ref)
        every = far_of(cut.per, h, all_ref, all_other_ref)
        sg_ref[h] = every + (own_ref[h] + near)
        if not masked:
            full = jnp.where(add_far, full, 0.0)
        suffix = full + jnp.where(add_near, near, 0.0)
        cols = cut.cols(h)
        for c in range(cut.chunks):
            rows = cut.rng(c)
            state = (suffix + after_ref[h, c]).astype(BF16)
            kg = kp_ref[cols, rows] + mm_rt(state, v_ref[rows, cols])
            vg = vp_ref[cols, rows] + mm_rt(state.T, k_ref[rows, cols])
            kg_ref[rows, cols] = kg.astype(BF16).T
            vg_ref[rows, cols] = vg.astype(BF16).T
        if final:
            at, to = pl.ds(h * cut.dim, cut.dim), pl.ds((cut.base + h) * cut.dim, cut.dim)
            copies += column_copies(
                [(kg_ref.at[:, at], kg_hbm.at[:, to]), (vg_ref.at[:, at], vg_hbm.at[:, to])],
                sems.at[h],
            )
    if final:
        copies += column_copies([(sg_ref, sg_hbm.at[pl.ds(cut.base, cut.per)])], sg_sem)
    for copy in copies:
        copy.wait()


def half_kernel(own_ref, near_ref, mine_ref):
    half = mine_ref.shape[0]
    first = lax.rem(lax.axis_index("ctx"), 2) == 0
    for h in range(half):
        mine_ref[h] = jnp.where(
            first, own_ref[h] + near_ref[h], own_ref[half + h] + near_ref[half + h]
        )


def shards(n, groups, queries, keys, values, init_state, out_grad):
    rows, width = queries.shape
    heads, dim = init_state.shape[:2]
    pairs = n // 2
    swap_pairs = [(i, i ^ 1) for i in range(n)]
    shift_pairs = [(i, (i + 2) % n) for i in range(n)]
    swap = lambda x: lax.ppermute(x, "ctx", swap_pairs)
    shift = lambda x: lax.ppermute(x, "ctx", shift_pairs)
    cuts = [Cut(rows, heads, dim, g, groups) for g in range(groups)]
    per, chunks, size = cuts[0].per, cuts[0].chunks, cuts[0].size
    wide_b = jax.ShapeDtypeStruct((rows, width), BF16)
    all_b = pltpu.VMEM((rows, width), BF16)
    part_b = pltpu.VMEM((rows, per * dim), BF16)
    part_f = pltpu.VMEM((rows, per * dim), F32)
    part_ft = pltpu.VMEM((per * dim, rows), F32)
    state_f = pltpu.VMEM((per, dim, dim), F32)
    states_f = pltpu.VMEM((per, chunks, dim, dim), F32)
    scores_b = pltpu.VMEM((per, chunks, size, size), BF16)
    small = 2 * per * rows * dim * dim
    square = 2 * per * rows * size * dim
    piece = rows * per * dim * 2
    dma = pltpu.SemaphoreType.DMA

    def call(body, name, ins, outs, scratch, flops, nbytes):
        return pl.pallas_call(
            body,
            in_specs=[VM] * len(ins),
            out_specs=[HB if isinstance(o, jax.ShapeDtypeStruct) else VM for o in outs],
            out_shape=list(outs),
            scratch_shapes=scratch,
            compiler_params=pltpu.CompilerParams(vmem_limit_bytes=16 * 1024 * 1024),
            cost_estimate=pl.CostEstimate(flops=flops, bytes_accessed=nbytes, transcendentals=0),
            name=name,
        )(*ins)

    def far_sums(mine, later):
        if pairs == 2:
            far = shift(mine)
            return far, far
        pair = lax.axis_index("ctx") // 2
        moving = mine
        used, every = jnp.zeros_like(mine), jnp.zeros_like(mine)
        for j in range(1, pairs):
            moving = shift(moving)
            wrapped = pair < j
            used = used + jnp.where(wrapped == later, moving, 0.0)
            every = every + moving
        return used, every

    def half_of(own, near):
        return pl.pallas_call(
            half_kernel,
            in_specs=[VM] * 2,
            out_specs=VM,
            out_shape=pltpu.VMEM((per // 2, dim, dim), F32),
            compiler_params=pltpu.CompilerParams(vmem_limit_bytes=4 * 1024 * 1024),
            name="half",
        )(own, near)

    masked = pairs != 2

    def state_call(g):
        order = keys if g == 0 else own[g - 1]
        return pl.pallas_call(
            functools.partial(state_kernel, cuts[g]),
            in_specs=[HB, HB, HB if g == 0 else VM],
            out_specs=[VM] * 4,
            out_shape=[state_f, states_f, part_b, part_b],
            scratch_shapes=[dma((2, per // 2))],
            compiler_params=pltpu.CompilerParams(vmem_limit_bytes=16 * 1024 * 1024),
            cost_estimate=pl.CostEstimate(
                flops=small, bytes_accessed=2 * piece, transcendentals=0
            ),
            name="states%d" % g,
        )(in_hbm(keys), in_hbm(values), in_hbm(order) if g == 0 else order)

    in_hbm = lambda x: pltpu.with_memory_space_constraint(x, pltpu.HBM)
    own, before, near, keys_v, values_v = {}, {}, {}, {}, {}
    for g, cut in enumerate(cuts):
        own[g], before[g], keys_v[g], values_v[g] = state_call(g)
        near[g] = swap(own[g])
    att, scores, queries_t, far, other = {}, {}, {}, {}, {}
    for g in range(groups):
        mine = half_of(own[g], near[g])
        far[g], _ = far_sums(mine, False)
        if g == groups - 1:
            mine, before[0] = lax.optimization_barrier((mine, before[0]))
    for g, cut in enumerate(cuts):
        att[g], scores[g], queries_t[g] = call(
            functools.partial(inner_kernel, cut),
            "inner%d" % g,
            [queries, keys_v[g], values_v[g], before[g]],
            [part_f, scores_b, pltpu.VMEM((per * dim, rows), BF16)],
            [],
            2 * square + small,
            0,
        )
    far[0], att[0], att[1] = lax.optimization_barrier((far[0], att[0], att[1]))
    for g in range(groups):
        other[g] = swap(far[g])
    out, ga, total, after, prefix = {}, {}, {}, {}, {}
    gnear, gfar, gall = {}, {}, {}
    for g, cut in enumerate(cuts):
        out[g], ga[g], total[g], after[g], prefix[g] = call(
            functools.partial(norm_kernel, cut, masked),
            "norm%d" % g,
            [att[g], queries, queries_t[g], out_grad, init_state, near[g], far[g], other[g]],
            [part_b, part_b, state_f, states_f, state_f],
            [],
            2 * small,
            piece,
        )
        gnear[g] = swap(total[g])
    gnear[0], total[1] = lax.optimization_barrier((gnear[0], total[1]))
    for g, cut in enumerate(cuts):
        gfar[g], gall[g] = far_sums(half_of(total[g], gnear[g]), True)
    kp, vp, qg = {}, {}, {}
    for g, cut in enumerate(cuts):
        ready = list(out.values()) if g == 0 else []
        qg[g], kp[g], vp[g], *written = call(
            functools.partial(back_kernel, cuts, g),
            "back%d" % g,
            [queries_t[g], keys_v[g], values_v[g], ga[g], prefix[g], before[g], scores[g], *ready],
            [part_b, part_ft, part_ft] + [wide_b] * (g == 0),
            [dma((groups,))] if g == 0 else [],
            4 * square + small,
            piece,
        )
        if g == 0:
            (output,) = written
        gfar[g], gall[g], kp[g] = lax.optimization_barrier((gfar[g], gall[g], kp[g]))
    ready = list(qg.values())
    for g, cut in enumerate(cuts):
        used = swap(gfar[g])
        total_far = used if pairs == 2 else swap(gall[g])
        ins = [
            keys_v[g], values_v[g], kp[g], vp[g], after[g], total[g], gnear[g],
            gfar[g], used, gall[g], total_far,
        ]
        outs, scratch = [part_b, part_b, state_f], []
        if g == groups - 1:
            scratch = outs + [dma((3 * g,)), dma((per, 2)), dma((1,))]
            outs = [wide_b, wide_b, jax.ShapeDtypeStruct(init_state.shape, F32)]
        elif g == 0:
            outs, scratch = outs + [wide_b], [dma((groups,))]
        ends = list(
            call(
                functools.partial(last_kernel, cuts, g, masked),
                "last%d" % g,
                ins + ready,
                outs,
                scratch,
                2 * small,
                2 * piece,
            )
        )
        if g == 0:
            ready, query_grad = [], ends.pop()
        ready += ends
    key_grad, value_grad, state_grad = ends
    return output, query_grad, key_grad, value_grad, state_grad


def solution(mesh):
    wide = P(("grp", "ctx"), "head")
    deep = P(("grp", "head"), None, None)
    return jax.shard_map(
        functools.partial(shards, mesh.shape["ctx"], 2),
        mesh=mesh,
        in_specs=(wide, wide, wide, deep, wide),
        out_specs=(wide, wide, wide, wide, deep),
        check_vma=False,
    )
```

```python
import functools

import jax
import jax.numpy as jnp
from jax import lax
from jax.experimental import pallas as pl
from jax.experimental.pallas import tpu as pltpu
from jax.sharding import PartitionSpec as P

F32 = jnp.float32
BF16 = jnp.bfloat16
EPS = 1e-06
VM = pl.BlockSpec(memory_space=pltpu.VMEM)
HB = pl.BlockSpec(memory_space=pltpu.HBM)


def mm(a, b):
    return lax.dot_general(a, b, (((1,), (0,)), ((), ())), preferred_element_type=F32)


def mm_rt(a, b):
    return lax.dot_general(a, b, (((1,), (1,)), ((), ())), preferred_element_type=F32)


def mm_lt(a, b):
    return lax.dot_general(a, b, (((0,), (0,)), ((), ())), preferred_element_type=F32)


def causal(size):
    return lax.broadcasted_iota(jnp.int32, (size, size), 0) >= lax.broadcasted_iota(
        jnp.int32, (size, size), 1
    )


class Cut:
    def __init__(self, rows, heads, dim, group, groups):
        self.rows, self.heads, self.dim = rows, heads, dim
        self.per = heads // groups
        self.base = group * self.per
        self.size = 256 if rows % 256 == 0 else rows
        self.chunks = rows // self.size

    def rng(self, c):
        return slice(c * self.size, (c + 1) * self.size)

    def cols(self, h):
        return slice(h * self.dim, (h + 1) * self.dim)

    def whole(self, h):
        return self.cols(self.base + h)

    def each(self):
        return [(h, c) for h in range(self.per) for c in range(self.chunks)]

    def span(self):
        return pl.ds(self.base * self.dim, self.per * self.dim)


def column_copies(pairs, sems):
    copies = [pltpu.make_async_copy(src, dst, sems.at[i]) for i, (src, dst) in enumerate(pairs)]
    for copy in copies:
        copy.start()
    return copies


def state_kernel(cut, k_hbm, v_hbm, _, total_ref, before_ref, k_ref, v_ref, sems):
    width = 2 * cut.dim

    def copy(i, j):
        src, dst = ((k_hbm, k_ref), (v_hbm, v_ref))[j]
        from_at = pl.ds(cut.base * cut.dim + i * width, width)
        return pltpu.make_async_copy(
            src.at[:, from_at], dst.at[:, pl.ds(i * width, width)], sems.at[j, i]
        )

    for i in range(cut.per // 2):
        copy(i, 0).start()
        copy(i, 1).start()
    for h in range(cut.per):
        if h % 2 == 0:
            copy(h // 2, 0).wait()
            copy(h // 2, 1).wait()
        terms = [
            mm_lt(k_ref[cut.rng(c), cut.cols(h)], v_ref[cut.rng(c), cut.cols(h)])
            for c in range(cut.chunks)
        ]
        run = jnp.zeros((cut.dim, cut.dim), F32)
        for c in range(cut.chunks):
            before_ref[h, c] = run
            run = run + terms[c]
        total_ref[h] = run


def inner_kernel(cut, q_ref, k_ref, v_ref, before_ref, att_ref, scores_ref, qt_ref):
    keep = causal(cut.size)
    each = cut.each()
    q = {(h, c): q_ref[cut.rng(c), cut.whole(h)] for h, c in each}
    k = {(h, c): k_ref[cut.rng(c), cut.cols(h)] for h, c in each}
    v = {(h, c): v_ref[cut.rng(c), cut.cols(h)] for h, c in each}
    scores = {j: jnp.where(keep, mm_rt(q[j], k[j]), 0.0).astype(BF16) for j in each}
    att = {j: mm(scores[j], v[j]) for j in each}
    for h, c in each:
        if c > 0:
            att[h, c] = att[h, c] + mm(q[h, c], before_ref[h, c].astype(BF16))
    for h, c in each:
        scores_ref[h, c] = scores[h, c]
        att_ref[cut.rng(c), cut.cols(h)] = att[h, c]
        qt_ref[cut.cols(h), cut.rng(c)] = q[h, c].T


def far_of(per, h, own_half, other_half):
    half = per // 2
    first = lax.rem(lax.axis_index("ctx"), 2) == 0
    mine, other = own_half[h % half], other_half[h % half]
    return jnp.where(first == (h < half), mine, other)


def norm_kernel(cut, masked, *refs):
    att_ref, q_ref, qt_ref, g_ref, init_ref, near_ref, far_ref, other_ref = refs[:8]
    out_ref, ga_ref, total_ref, after_ref, prefix_ref = refs[8:]
    place = lax.axis_index("ctx")
    add_near = lax.rem(place, 2) == 1
    add_far = place >= 2
    for h in range(cut.per):
        full = far_of(cut.per, h, far_ref, other_ref)
        if not masked:
            full = jnp.where(add_far, full, 0.0)
        prefix_ref[h] = init_ref[cut.base + h] + (full + jnp.where(add_near, near_ref[h], 0.0))
    for h in range(cut.per):
        att = att_ref[:, cut.cols(h)] + mm(q_ref[:, cut.whole(h)], prefix_ref[h].astype(BF16))
        ga = []
        for c in range(cut.chunks):
            x = att[cut.rng(c)]
            up = g_ref[cut.rng(c), cut.whole(h)].astype(F32)
            square = jnp.sum(x * x, axis=-1, keepdims=True)
            along = jnp.sum(up * x, axis=-1, keepdims=True)
            inv = lax.rsqrt(square * (1.0 / cut.dim) + EPS)
            normed = x * inv
            ga.append((inv * (up - normed * (along * (inv * (1.0 / cut.dim))))).astype(BF16))
            out_ref[cut.rng(c), cut.cols(h)] = normed.astype(BF16)
            ga_ref[cut.rng(c), cut.cols(h)] = ga[c]
        run = jnp.zeros((cut.dim, cut.dim), F32)
        for c in reversed(range(cut.chunks)):
            after_ref[h, c] = run
            run = run + mm(qt_ref[cut.cols(h), cut.rng(c)], ga[c])
        total_ref[h] = run


def back_kernel(cuts, g, *refs):
    cut = cuts[g]
    count = len(cuts) if g == 0 else 0
    qt_ref, k_ref, v_ref, ga_ref, prefix_ref, before_ref, scores_ref = refs[:7]
    ready = refs[7 : 7 + count]
    qg_ref, kg_ref, vg_ref = refs[7 + count : 10 + count]
    copies = []
    if g == 0:
        hbm, sems = refs[10 + count :]
        copies = column_copies([(r, hbm.at[:, cuts[i].span()]) for i, r in enumerate(ready)], sems)
    keep = causal(cut.size)
    each = cut.each()
    qt = {j: qt_ref[cut.cols(j[0]), cut.rng(j[1])] for j in each}
    k = {j: k_ref[cut.rng(j[1]), cut.cols(j[0])] for j in each}
    v = {j: v_ref[cut.rng(j[1]), cut.cols(j[0])] for j in each}
    ga = {j: ga_ref[cut.rng(j[1]), cut.cols(j[0])] for j in each}
    state = {
        (h, c): (prefix_ref[h] + before_ref[h, c]).astype(BF16) for h, c in each
    }
    scores = {j: scores_ref[j[0], j[1]] for j in each}
    grad = {j: jnp.where(keep, mm_rt(ga[j], v[j]), 0.0).astype(BF16) for j in each}
    qg = {j: mm(grad[j], k[j]) + mm_rt(ga[j], state[j]) for j in each}
    for h, c in each:
        qg_ref[cut.rng(c), cut.cols(h)] = qg[h, c].astype(BF16)
    vg = {j: mm(ga[j].T, scores[j]) for j in each}
    kg = {j: mm(qt[j], grad[j]) for j in each}
    for h, c in each:
        kg_ref[cut.cols(h), cut.rng(c)] = kg[h, c]
        vg_ref[cut.cols(h), cut.rng(c)] = vg[h, c]
    for copy in copies:
        copy.wait()


def last_kernel(cuts, g, masked, *refs):
    cut = cuts[g]
    k_ref, v_ref, kp_ref, vp_ref, after_ref, own_ref, near_ref = refs[:7]
    far_ref, other_ref, all_ref, all_other_ref = refs[7:11]
    final = g == len(cuts) - 1
    ready, refs = [refs[11 + 3 * i : 14 + 3 * i] for i in range(g)], refs[11 + 3 * g :]
    if final:
        grads, refs = refs[: len(cuts)], refs[len(cuts) :]
    if final:
        kg_hbm, vg_hbm, sg_hbm, hbm, kg_ref, vg_ref, sg_ref, ready_sems, sems, sg_sem, qg_sems = refs
    else:
        kg_ref, vg_ref, sg_ref = refs
    place = lax.axis_index("ctx")
    add_near = lax.rem(place, 2) == 0
    add_far = place < 2
    copies = []
    if final:
        copies += column_copies(
            [(r, hbm.at[:, cuts[i].span()]) for i, r in enumerate(grads)], qg_sems
        )
    if final:
        pairs = []
        for i, (kg, vg, sg) in enumerate(ready):
            at = cuts[i].span()
            pairs += [(kg, kg_hbm.at[:, at]), (vg, vg_hbm.at[:, at])]
            pairs += [(sg, sg_hbm.at[pl.ds(cuts[i].base, cut.per)])]
        copies += column_copies(pairs, ready_sems)
    for h in range(cut.per):
        near = near_ref[h]
        full = far_of(cut.per, h, far_ref, other_ref)
        every = far_of(cut.per, h, all_ref, all_other_ref)
        sg_ref[h] = every + (own_ref[h] + near)
        if not masked:
            full = jnp.where(add_far, full, 0.0)
        suffix = full + jnp.where(add_near, near, 0.0)
        cols = cut.cols(h)
        for c in range(cut.chunks):
            rows = cut.rng(c)
            state = (suffix + after_ref[h, c]).astype(BF16)
            kg = kp_ref[cols, rows] + mm_rt(state, v_ref[rows, cols])
            vg = vp_ref[cols, rows] + mm_rt(state.T, k_ref[rows, cols])
            kg_ref[rows, cols] = kg.astype(BF16).T
            vg_ref[rows, cols] = vg.astype(BF16).T
        if final:
            at, to = pl.ds(h * cut.dim, cut.dim), pl.ds((cut.base + h) * cut.dim, cut.dim)
            copies += column_copies(
                [(kg_ref.at[:, at], kg_hbm.at[:, to]), (vg_ref.at[:, at], vg_hbm.at[:, to])],
                sems.at[h],
            )
    if final:
        copies += column_copies([(sg_ref, sg_hbm.at[pl.ds(cut.base, cut.per)])], sg_sem)
    for copy in copies:
        copy.wait()


def half_kernel(own_ref, near_ref, mine_ref):
    half = mine_ref.shape[0]
    first = lax.rem(lax.axis_index("ctx"), 2) == 0
    for h in range(half):
        mine_ref[h] = jnp.where(
            first, own_ref[h] + near_ref[h], own_ref[half + h] + near_ref[half + h]
        )


def shards(n, groups, queries, keys, values, init_state, out_grad):
    rows, width = queries.shape
    heads, dim = init_state.shape[:2]
    pairs = n // 2
    swap_pairs = [(i, i ^ 1) for i in range(n)]
    shift_pairs = [(i, (i + 2) % n) for i in range(n)]
    swap = lambda x: lax.ppermute(x, "ctx", swap_pairs)
    shift = lambda x: lax.ppermute(x, "ctx", shift_pairs)
    cuts = [Cut(rows, heads, dim, g, groups) for g in range(groups)]
    per, chunks, size = cuts[0].per, cuts[0].chunks, cuts[0].size
    wide_b = jax.ShapeDtypeStruct((rows, width), BF16)
    all_b = pltpu.VMEM((rows, width), BF16)
    part_b = pltpu.VMEM((rows, per * dim), BF16)
    part_f = pltpu.VMEM((rows, per * dim), F32)
    part_ft = pltpu.VMEM((per * dim, rows), F32)
    state_f = pltpu.VMEM((per, dim, dim), F32)
    states_f = pltpu.VMEM((per, chunks, dim, dim), F32)
    scores_b = pltpu.VMEM((per, chunks, size, size), BF16)
    small = 2 * per * rows * dim * dim
    square = 2 * per * rows * size * dim
    piece = rows * per * dim * 2
    dma = pltpu.SemaphoreType.DMA

    def call(body, name, ins, outs, scratch, flops, nbytes):
        return pl.pallas_call(
            body,
            in_specs=[VM] * len(ins),
            out_specs=[HB if isinstance(o, jax.ShapeDtypeStruct) else VM for o in outs],
            out_shape=list(outs),
            scratch_shapes=scratch,
            compiler_params=pltpu.CompilerParams(vmem_limit_bytes=16 * 1024 * 1024),
            cost_estimate=pl.CostEstimate(flops=flops, bytes_accessed=nbytes, transcendentals=0),
            name=name,
        )(*ins)

    def far_sums(mine, later):
        if pairs == 2:
            far = shift(mine)
            return far, far
        pair = lax.axis_index("ctx") // 2
        moving = mine
        used, every = jnp.zeros_like(mine), jnp.zeros_like(mine)
        for j in range(1, pairs):
            moving = shift(moving)
            wrapped = pair < j
            used = used + jnp.where(wrapped == later, moving, 0.0)
            every = every + moving
        return used, every

    def half_of(own, near):
        return pl.pallas_call(
            half_kernel,
            in_specs=[VM] * 2,
            out_specs=VM,
            out_shape=pltpu.VMEM((per // 2, dim, dim), F32),
            compiler_params=pltpu.CompilerParams(vmem_limit_bytes=4 * 1024 * 1024),
            name="half",
        )(own, near)

    masked = pairs != 2

    def state_call(g):
        order = keys if g == 0 else own[g - 1]
        return pl.pallas_call(
            functools.partial(state_kernel, cuts[g]),
            in_specs=[HB, HB, HB if g == 0 else VM],
            out_specs=[VM] * 4,
            out_shape=[state_f, states_f, part_b, part_b],
            scratch_shapes=[dma((2, per // 2))],
            compiler_params=pltpu.CompilerParams(vmem_limit_bytes=16 * 1024 * 1024),
            cost_estimate=pl.CostEstimate(
                flops=small, bytes_accessed=2 * piece, transcendentals=0
            ),
            name="states%d" % g,
        )(in_hbm(keys), in_hbm(values), in_hbm(order) if g == 0 else order)

    in_hbm = lambda x: pltpu.with_memory_space_constraint(x, pltpu.HBM)
    own, before, near, keys_v, values_v = {}, {}, {}, {}, {}
    for g, cut in enumerate(cuts):
        own[g], before[g], keys_v[g], values_v[g] = state_call(g)
        near[g] = swap(own[g])
    att, scores, queries_t, far, other = {}, {}, {}, {}, {}
    for g in range(groups):
        mine = half_of(own[g], near[g])
        far[g], _ = far_sums(mine, False)
        if g == groups - 1:
            mine, before[0] = lax.optimization_barrier((mine, before[0]))
    for g, cut in enumerate(cuts):
        att[g], scores[g], queries_t[g] = call(
            functools.partial(inner_kernel, cut),
            "inner%d" % g,
            [queries, keys_v[g], values_v[g], before[g]],
            [part_f, scores_b, pltpu.VMEM((per * dim, rows), BF16)],
            [],
            2 * square + small,
            0,
        )
    far[0], att[0], att[1] = lax.optimization_barrier((far[0], att[0], att[1]))
    for g in range(groups):
        other[g] = swap(far[g])
    out, ga, total, after, prefix = {}, {}, {}, {}, {}
    gnear, gfar, gall = {}, {}, {}
    for g, cut in enumerate(cuts):
        out[g], ga[g], total[g], after[g], prefix[g] = call(
            functools.partial(norm_kernel, cut, masked),
            "norm%d" % g,
            [att[g], queries, queries_t[g], out_grad, init_state, near[g], far[g], other[g]],
            [part_b, part_b, state_f, states_f, state_f],
            [],
            2 * small,
            piece,
        )
        gnear[g] = swap(total[g])
    gnear[0], total[1] = lax.optimization_barrier((gnear[0], total[1]))
    for g, cut in enumerate(cuts):
        gfar[g], gall[g] = far_sums(half_of(total[g], gnear[g]), True)
    kp, vp, qg = {}, {}, {}
    for g, cut in enumerate(cuts):
        ready = list(out.values()) if g == 0 else []
        qg[g], kp[g], vp[g], *written = call(
            functools.partial(back_kernel, cuts, g),
            "back%d" % g,
            [queries_t[g], keys_v[g], values_v[g], ga[g], prefix[g], before[g], scores[g], *ready],
            [part_b, part_ft, part_ft] + [wide_b] * (g == 0),
            [dma((groups,))] if g == 0 else [],
            4 * square + small,
            piece,
        )
        if g == 0:
            (output,) = written
        gfar[g], gall[g], kp[g] = lax.optimization_barrier((gfar[g], gall[g], kp[g]))
    ready = []
    for g, cut in enumerate(cuts):
        used = swap(gfar[g])
        total_far = used if pairs == 2 else swap(gall[g])
        ins = [
            keys_v[g], values_v[g], kp[g], vp[g], after[g], total[g], gnear[g],
            gfar[g], used, gall[g], total_far,
        ]
        outs, scratch = [part_b, part_b, state_f], []
        if g == groups - 1:
            scratch = outs + [dma((3 * g,)), dma((per, 2)), dma((1,)), dma((groups,))]
            outs = [wide_b, wide_b, jax.ShapeDtypeStruct(init_state.shape, F32), wide_b]
            ready += list(qg.values())
        ends = list(
            call(
                functools.partial(last_kernel, cuts, g, masked),
                "last%d" % g,
                ins + ready,
                outs,
                scratch,
                2 * small,
                2 * piece,
            )
        )
        ready += ends
    key_grad, value_grad, state_grad, query_grad = ends
    return output, query_grad, key_grad, value_grad, state_grad


def solution(mesh):
    wide = P(("grp", "ctx"), "head")
    deep = P(("grp", "head"), None, None)
    return jax.shard_map(
        functools.partial(shards, mesh.shape["ctx"], 2),
        mesh=mesh,
        in_specs=(wide, wide, wide, deep, wide),
        out_specs=(wide, wide, wide, wide, deep),
        check_vma=False,
    )
```

```python
import functools

import jax
import jax.numpy as jnp
from jax import lax
from jax.experimental import pallas as pl
from jax.experimental.pallas import tpu as pltpu
from jax.sharding import PartitionSpec as P

F32 = jnp.float32
BF16 = jnp.bfloat16
EPS = 1e-06
VM = pl.BlockSpec(memory_space=pltpu.VMEM)
HB = pl.BlockSpec(memory_space=pltpu.HBM)


def mm(a, b):
    return lax.dot_general(a, b, (((1,), (0,)), ((), ())), preferred_element_type=F32)


def mm_rt(a, b):
    return lax.dot_general(a, b, (((1,), (1,)), ((), ())), preferred_element_type=F32)


def mm_lt(a, b):
    return lax.dot_general(a, b, (((0,), (0,)), ((), ())), preferred_element_type=F32)


def causal(size):
    return lax.broadcasted_iota(jnp.int32, (size, size), 0) >= lax.broadcasted_iota(
        jnp.int32, (size, size), 1
    )


class Cut:
    def __init__(self, rows, heads, dim, group, groups):
        self.rows, self.heads, self.dim = rows, heads, dim
        self.per = heads // groups
        self.base = group * self.per
        self.size = 256 if rows % 256 == 0 else rows
        self.chunks = rows // self.size

    def rng(self, c):
        return slice(c * self.size, (c + 1) * self.size)

    def cols(self, h):
        return slice(h * self.dim, (h + 1) * self.dim)

    def whole(self, h):
        return self.cols(self.base + h)

    def each(self):
        return [(h, c) for h in range(self.per) for c in range(self.chunks)]

    def span(self):
        return pl.ds(self.base * self.dim, self.per * self.dim)


def column_copies(pairs, sems):
    copies = [pltpu.make_async_copy(src, dst, sems.at[i]) for i, (src, dst) in enumerate(pairs)]
    for copy in copies:
        copy.start()
    return copies


def state_kernel(cut, k_hbm, v_hbm, _, total_ref, before_ref, k_ref, v_ref, sems):
    width = 2 * cut.dim

    def copy(i, j):
        src, dst = ((k_hbm, k_ref), (v_hbm, v_ref))[j]
        from_at = pl.ds(cut.base * cut.dim + i * width, width)
        return pltpu.make_async_copy(
            src.at[:, from_at], dst.at[:, pl.ds(i * width, width)], sems.at[j, i]
        )

    for i in range(cut.per // 2):
        copy(i, 0).start()
        copy(i, 1).start()
    for h in range(cut.per):
        if h % 2 == 0:
            copy(h // 2, 0).wait()
            copy(h // 2, 1).wait()
        terms = [
            mm_lt(k_ref[cut.rng(c), cut.cols(h)], v_ref[cut.rng(c), cut.cols(h)])
            for c in range(cut.chunks)
        ]
        run = jnp.zeros((cut.dim, cut.dim), F32)
        for c in range(cut.chunks):
            before_ref[h, c] = run
            run = run + terms[c]
        total_ref[h] = run


def inner_kernel(cut, q_ref, k_ref, v_ref, before_ref, att_ref, scores_ref, qt_ref):
    keep = causal(cut.size)
    each = cut.each()
    q = {(h, c): q_ref[cut.rng(c), cut.whole(h)] for h, c in each}
    k = {(h, c): k_ref[cut.rng(c), cut.cols(h)] for h, c in each}
    v = {(h, c): v_ref[cut.rng(c), cut.cols(h)] for h, c in each}
    scores = {j: jnp.where(keep, mm_rt(q[j], k[j]), 0.0).astype(BF16) for j in each}
    att = {j: mm(scores[j], v[j]) for j in each}
    for h, c in each:
        if c > 0:
            att[h, c] = att[h, c] + mm(q[h, c], before_ref[h, c].astype(BF16))
    for h, c in each:
        scores_ref[h, c] = scores[h, c]
        att_ref[cut.rng(c), cut.cols(h)] = att[h, c]
        qt_ref[cut.cols(h), cut.rng(c)] = q[h, c].T


def far_of(per, h, own_half, other_half):
    half = per // 2
    first = lax.rem(lax.axis_index("ctx"), 2) == 0
    mine, other = own_half[h % half], other_half[h % half]
    return jnp.where(first == (h < half), mine, other)


def norm_kernel(cut, masked, *refs):
    att_ref, q_ref, qt_ref, g_ref, init_ref, near_ref, far_ref, other_ref = refs[:8]
    out_ref, ga_ref, total_ref, after_ref, prefix_ref = refs[8:]
    place = lax.axis_index("ctx")
    add_near = lax.rem(place, 2) == 1
    add_far = place >= 2
    for h in range(cut.per):
        full = far_of(cut.per, h, far_ref, other_ref)
        if not masked:
            full = jnp.where(add_far, full, 0.0)
        prefix_ref[h] = init_ref[cut.base + h] + (full + jnp.where(add_near, near_ref[h], 0.0))
    for h in range(cut.per):
        att = att_ref[:, cut.cols(h)] + mm(q_ref[:, cut.whole(h)], prefix_ref[h].astype(BF16))
        ga = []
        for c in range(cut.chunks):
            x = att[cut.rng(c)]
            up = g_ref[cut.rng(c), cut.whole(h)].astype(F32)
            square = jnp.sum(x * x, axis=-1, keepdims=True)
            along = jnp.sum(up * x, axis=-1, keepdims=True)
            inv = lax.rsqrt(square * (1.0 / cut.dim) + EPS)
            normed = x * inv
            ga.append((inv * (up - normed * (along * (inv * (1.0 / cut.dim))))).astype(BF16))
            out_ref[cut.rng(c), cut.cols(h)] = normed.astype(BF16)
            ga_ref[cut.rng(c), cut.cols(h)] = ga[c]
        run = jnp.zeros((cut.dim, cut.dim), F32)
        for c in reversed(range(cut.chunks)):
            after_ref[h, c] = run
            run = run + mm(qt_ref[cut.cols(h), cut.rng(c)], ga[c])
        total_ref[h] = run


def back_kernel(cuts, g, *refs):
    cut = cuts[g]
    count = len(cuts) if g == 0 else 0
    qt_ref, k_ref, v_ref, ga_ref, prefix_ref, before_ref, scores_ref = refs[:7]
    ready = refs[7 : 7 + count]
    qg_ref, kg_ref, vg_ref = refs[7 + count : 10 + count]
    copies = []
    if g == 0:
        hbm, sems = refs[10 + count :]
        copies = column_copies([(r, hbm.at[:, cuts[i].span()]) for i, r in enumerate(ready)], sems)
    keep = causal(cut.size)
    each = cut.each()
    qt = {j: qt_ref[cut.cols(j[0]), cut.rng(j[1])] for j in each}
    k = {j: k_ref[cut.rng(j[1]), cut.cols(j[0])] for j in each}
    v = {j: v_ref[cut.rng(j[1]), cut.cols(j[0])] for j in each}
    ga = {j: ga_ref[cut.rng(j[1]), cut.cols(j[0])] for j in each}
    state = {
        (h, c): (prefix_ref[h] + before_ref[h, c]).astype(BF16) for h, c in each
    }
    scores = {j: scores_ref[j[0], j[1]] for j in each}
    grad = {j: jnp.where(keep, mm_rt(ga[j], v[j]), 0.0).astype(BF16) for j in each}
    qg = {j: mm(grad[j], k[j]) + mm_rt(ga[j], state[j]) for j in each}
    for h, c in each:
        qg_ref[cut.rng(c), cut.cols(h)] = qg[h, c].astype(BF16)
    vg = {j: mm(ga[j].T, scores[j]) for j in each}
    kg = {j: mm(qt[j], grad[j]) for j in each}
    for h, c in each:
        kg_ref[cut.cols(h), cut.rng(c)] = kg[h, c]
        vg_ref[cut.cols(h), cut.rng(c)] = vg[h, c]
    for copy in copies:
        copy.wait()


def last_kernel(cuts, g, masked, *refs):
    cut = cuts[g]
    k_ref, v_ref, kp_ref, vp_ref, after_ref, own_ref, near_ref = refs[:7]
    far_ref, other_ref, all_ref, all_other_ref = refs[7:11]
    final = g == len(cuts) - 1
    ready, refs = [refs[11 + 3 * i : 14 + 3 * i] for i in range(g)], refs[11 + 3 * g :]
    if final:
        grads, refs = refs[: len(cuts)], refs[len(cuts) :]
    if final:
        kg_hbm, vg_hbm, sg_hbm, hbm, kg_ref, vg_ref, sg_ref, ready_sems, sems, sg_sem, qg_sems = refs
    else:
        kg_ref, vg_ref, sg_ref = refs
    place = lax.axis_index("ctx")
    add_near = lax.rem(place, 2) == 0
    add_far = place < 2
    copies = []
    if final:
        copies += column_copies(
            [(r, hbm.at[:, cuts[i].span()]) for i, r in enumerate(grads)], qg_sems
        )
    if final:
        pairs = []
        for i, (kg, vg, sg) in enumerate(ready):
            at = cuts[i].span()
            pairs += [(kg, kg_hbm.at[:, at]), (vg, vg_hbm.at[:, at])]
            pairs += [(sg, sg_hbm.at[pl.ds(cuts[i].base, cut.per)])]
        copies += column_copies(pairs, ready_sems)
    for h in range(cut.per):
        near = near_ref[h]
        full = far_of(cut.per, h, far_ref, other_ref)
        every = far_of(cut.per, h, all_ref, all_other_ref)
        sg_ref[h] = every + (own_ref[h] + near)
        if not masked:
            full = jnp.where(add_far, full, 0.0)
        suffix = full + jnp.where(add_near, near, 0.0)
        cols = cut.cols(h)
        for c in range(cut.chunks):
            rows = cut.rng(c)
            state = (suffix + after_ref[h, c]).astype(BF16)
            kg = kp_ref[cols, rows] + mm_rt(state, v_ref[rows, cols])
            vg = vp_ref[cols, rows] + mm_rt(state.T, k_ref[rows, cols])
            kg_ref[rows, cols] = kg.astype(BF16).T
            vg_ref[rows, cols] = vg.astype(BF16).T
            if final and (c == cut.chunks - 1 or (h == cut.per - 1 and c == cut.chunks // 2 - 1)):
                split = h == cut.per - 1 and cut.chunks > 1
                start = cut.chunks // 2 if split and c == cut.chunks - 1 else 0
                span = pl.ds(start * cut.size, (c + 1 - start) * cut.size)
                at, to = pl.ds(h * cut.dim, cut.dim), pl.ds((cut.base + h) * cut.dim, cut.dim)
                copies += column_copies(
                    [
                        (kg_ref.at[span, at], kg_hbm.at[span, to]),
                        (vg_ref.at[span, at], vg_hbm.at[span, to]),
                    ],
                    sems.at[h + (start > 0)],
                )
    if final:
        copies += column_copies([(sg_ref, sg_hbm.at[pl.ds(cut.base, cut.per)])], sg_sem)
    for copy in copies:
        copy.wait()


def half_kernel(own_ref, near_ref, mine_ref):
    half = mine_ref.shape[0]
    first = lax.rem(lax.axis_index("ctx"), 2) == 0
    for h in range(half):
        mine_ref[h] = jnp.where(
            first, own_ref[h] + near_ref[h], own_ref[half + h] + near_ref[half + h]
        )


def shards(n, groups, queries, keys, values, init_state, out_grad):
    rows, width = queries.shape
    heads, dim = init_state.shape[:2]
    pairs = n // 2
    swap_pairs = [(i, i ^ 1) for i in range(n)]
    shift_pairs = [(i, (i + 2) % n) for i in range(n)]
    swap = lambda x: lax.ppermute(x, "ctx", swap_pairs)
    shift = lambda x: lax.ppermute(x, "ctx", shift_pairs)
    cuts = [Cut(rows, heads, dim, g, groups) for g in range(groups)]
    per, chunks, size = cuts[0].per, cuts[0].chunks, cuts[0].size
    wide_b = jax.ShapeDtypeStruct((rows, width), BF16)
    all_b = pltpu.VMEM((rows, width), BF16)
    part_b = pltpu.VMEM((rows, per * dim), BF16)
    part_f = pltpu.VMEM((rows, per * dim), F32)
    part_ft = pltpu.VMEM((per * dim, rows), F32)
    state_f = pltpu.VMEM((per, dim, dim), F32)
    states_f = pltpu.VMEM((per, chunks, dim, dim), F32)
    scores_b = pltpu.VMEM((per, chunks, size, size), BF16)
    small = 2 * per * rows * dim * dim
    square = 2 * per * rows * size * dim
    piece = rows * per * dim * 2
    dma = pltpu.SemaphoreType.DMA

    def call(body, name, ins, outs, scratch, flops, nbytes):
        return pl.pallas_call(
            body,
            in_specs=[VM] * len(ins),
            out_specs=[HB if isinstance(o, jax.ShapeDtypeStruct) else VM for o in outs],
            out_shape=list(outs),
            scratch_shapes=scratch,
            compiler_params=pltpu.CompilerParams(vmem_limit_bytes=16 * 1024 * 1024),
            cost_estimate=pl.CostEstimate(flops=flops, bytes_accessed=nbytes, transcendentals=0),
            name=name,
        )(*ins)

    def far_sums(mine, later):
        if pairs == 2:
            far = shift(mine)
            return far, far
        pair = lax.axis_index("ctx") // 2
        moving = mine
        used, every = jnp.zeros_like(mine), jnp.zeros_like(mine)
        for j in range(1, pairs):
            moving = shift(moving)
            wrapped = pair < j
            used = used + jnp.where(wrapped == later, moving, 0.0)
            every = every + moving
        return used, every

    def half_of(own, near):
        return pl.pallas_call(
            half_kernel,
            in_specs=[VM] * 2,
            out_specs=VM,
            out_shape=pltpu.VMEM((per // 2, dim, dim), F32),
            compiler_params=pltpu.CompilerParams(vmem_limit_bytes=4 * 1024 * 1024),
            name="half",
        )(own, near)

    masked = pairs != 2

    def state_call(g):
        order = keys if g == 0 else own[g - 1]
        return pl.pallas_call(
            functools.partial(state_kernel, cuts[g]),
            in_specs=[HB, HB, HB if g == 0 else VM],
            out_specs=[VM] * 4,
            out_shape=[state_f, states_f, part_b, part_b],
            scratch_shapes=[dma((2, per // 2))],
            compiler_params=pltpu.CompilerParams(vmem_limit_bytes=16 * 1024 * 1024),
            cost_estimate=pl.CostEstimate(
                flops=small, bytes_accessed=2 * piece, transcendentals=0
            ),
            name="states%d" % g,
        )(in_hbm(keys), in_hbm(values), in_hbm(order) if g == 0 else order)

    in_hbm = lambda x: pltpu.with_memory_space_constraint(x, pltpu.HBM)
    own, before, near, keys_v, values_v = {}, {}, {}, {}, {}
    for g, cut in enumerate(cuts):
        own[g], before[g], keys_v[g], values_v[g] = state_call(g)
        near[g] = swap(own[g])
    att, scores, queries_t, far, other = {}, {}, {}, {}, {}
    for g in range(groups):
        mine = half_of(own[g], near[g])
        far[g], _ = far_sums(mine, False)
        if g == groups - 1:
            mine, before[0] = lax.optimization_barrier((mine, before[0]))
    for g, cut in enumerate(cuts):
        att[g], scores[g], queries_t[g] = call(
            functools.partial(inner_kernel, cut),
            "inner%d" % g,
            [queries, keys_v[g], values_v[g], before[g]],
            [part_f, scores_b, pltpu.VMEM((per * dim, rows), BF16)],
            [],
            2 * square + small,
            0,
        )
    far[0], att[0], att[1] = lax.optimization_barrier((far[0], att[0], att[1]))
    for g in range(groups):
        other[g] = swap(far[g])
    out, ga, total, after, prefix = {}, {}, {}, {}, {}
    gnear, gfar, gall = {}, {}, {}
    for g, cut in enumerate(cuts):
        out[g], ga[g], total[g], after[g], prefix[g] = call(
            functools.partial(norm_kernel, cut, masked),
            "norm%d" % g,
            [att[g], queries, queries_t[g], out_grad, init_state, near[g], far[g], other[g]],
            [part_b, part_b, state_f, states_f, state_f],
            [],
            2 * small,
            piece,
        )
        gnear[g] = swap(total[g])
    gnear[0], total[1] = lax.optimization_barrier((gnear[0], total[1]))
    for g, cut in enumerate(cuts):
        gfar[g], gall[g] = far_sums(half_of(total[g], gnear[g]), True)
    kp, vp, qg = {}, {}, {}
    for g, cut in enumerate(cuts):
        ready = list(out.values()) if g == 0 else []
        qg[g], kp[g], vp[g], *written = call(
            functools.partial(back_kernel, cuts, g),
            "back%d" % g,
            [queries_t[g], keys_v[g], values_v[g], ga[g], prefix[g], before[g], scores[g], *ready],
            [part_b, part_ft, part_ft] + [wide_b] * (g == 0),
            [dma((groups,))] if g == 0 else [],
            4 * square + small,
            piece,
        )
        if g == 0:
            (output,) = written
        gfar[g], gall[g], kp[g] = lax.optimization_barrier((gfar[g], gall[g], kp[g]))
    ready = []
    for g, cut in enumerate(cuts):
        used = swap(gfar[g])
        total_far = used if pairs == 2 else swap(gall[g])
        ins = [
            keys_v[g], values_v[g], kp[g], vp[g], after[g], total[g], gnear[g],
            gfar[g], used, gall[g], total_far,
        ]
        outs, scratch = [part_b, part_b, state_f], []
        if g == groups - 1:
            scratch = outs + [dma((3 * g,)), dma((per + 1, 2)), dma((1,)), dma((groups,))]
            outs = [wide_b, wide_b, jax.ShapeDtypeStruct(init_state.shape, F32), wide_b]
            ready += list(qg.values())
        ends = list(
            call(
                functools.partial(last_kernel, cuts, g, masked),
                "last%d" % g,
                ins + ready,
                outs,
                scratch,
                2 * small,
                2 * piece,
            )
        )
        ready += ends
    key_grad, value_grad, state_grad, query_grad = ends
    return output, query_grad, key_grad, value_grad, state_grad


def solution(mesh):
    wide = P(("grp", "ctx"), "head")
    deep = P(("grp", "head"), None, None)
    return jax.shard_map(
        functools.partial(shards, mesh.shape["ctx"], 2),
        mesh=mesh,
        in_specs=(wide, wide, wide, deep, wide),
        out_specs=(wide, wide, wide, wide, deep),
        check_vma=False,
    )
```
